32 devices in a mesh: seq: 8 (over z, x), head: 4 (over y, core).
Axes of the slice: x: 2, y: 2, z: 4, core: 2. Of those that a mesh axis runs over, the one named last changes fastest.
Arguments:
- queries: bfloat16 [4096, 2048], P('seq', 'head'), may hold values from -12 to 12
- keys: bfloat16 [4096, 2048], P('seq', 'head'), may hold values from -12 to 12
- values: bfloat16 [4096, 2048], P('seq', 'head'), may hold values from -6 to 6
- cluster_ids: int32 [16, 4096], P('head', 'seq'), may hold values from 0 to 255, as said below
- out_weight: bfloat16 [2048, 2048], P('head'), may hold values from -0.5 to 0.5
Outputs:
- mixed: bfloat16 [4096, 2048], P('seq', 'head')
The draws below stay inside these ranges and needn't reach their ends.
Inputs may be any that keep to these rules, and one draw needn't show every extreme that they name: `cluster_ids`: within one head, the 512 tokens of one aligned block name no cluster more than 4 times, and in every block some cluster exactly 4 times.
All inputs are finite; a program needn't handle non-finite values.
Results may differ from the reference program's by a relative error of at most 0.0055.
Values may be sent and summed in bfloat16 or wider, within the bound.
No kernel may reach another device: no remote copies, remote signals or barrier semaphores. Data moves between devices by JAX's collectives and lax.ppermute only.
A program may use at most 64 MiB of HBM per device.

```python
import math
import jax
import jax.numpy as jnp
from jax import lax

D = 2048
HEADS = 16
HD = 128
CLUSTERS = 256
MOST = 4
TOK_DEV = 512
TOKENS = 4096
BLOCK = 32


def cluster_plan(key):
    blocks = TOKENS // TOK_DEV
    slot_total = CLUSTERS * MOST
    popular = jax.random.randint(jax.random.fold_in(key, 101), (HEADS, 1, CLUSTERS, 1), 0, 4)
    chosen = jax.random.randint(jax.random.fold_in(key, 102), (HEADS, blocks, 1, 1), 0, CLUSTERS)
    noise = jax.random.randint(jax.random.fold_in(key, 103), (HEADS, blocks, CLUSTERS, MOST), 0, 1024)
    cluster_axis = jnp.arange(CLUSTERS, dtype=jnp.int32)[None, None, :, None]
    level = noise + 300 * popular + 8192 * (cluster_axis == chosen).astype(jnp.int32)
    level = level.reshape(HEADS, blocks, slot_total) * slot_total + jnp.arange(slot_total, dtype=jnp.int32)
    picked = lax.top_k(level, TOK_DEV)[1]
    named = (picked // MOST).astype(jnp.int32)
    order_keys = jax.random.split(jax.random.fold_in(key, 104), HEADS * blocks)
    orders = jax.vmap(lambda single: jax.random.permutation(single, TOK_DEV))(order_keys).reshape(HEADS, blocks, TOK_DEV)
    named = jnp.take_along_axis(named, orders, axis=2)
    return named.reshape(HEADS, TOKENS)


def attention_draw(own_key):
    base = jnp.clip(jax.random.normal(own_key, (HEADS, TOKENS, HD), jnp.float32), -6.0, 6.0)
    return jnp.transpose(base, (1, 0, 2)).reshape(TOKENS, HEADS * HD)


def draw_queries(key, part):
    own_key = jax.random.fold_in(key, 11)
    return attention_draw(own_key).astype(jnp.bfloat16)


def draw_keys(key, part):
    own_key = jax.random.fold_in(key, 12)
    return attention_draw(own_key).astype(jnp.bfloat16)


def draw_cluster_ids(key, part):
    named = cluster_plan(key)
    return named


def block_scale(key, extent, cuts, low, largest):
    def one(dim, shards_of):
        draws = jax.random.uniform(jax.random.fold_in(jax.random.fold_in(key, 6), dim), (shards_of,), jnp.float32, low / len(cuts), largest / len(cuts))
        return jnp.repeat(jnp.exp(draws), extent[dim] // shards_of).reshape((-1,) + (1,) * (len(extent) - dim - 1))

    loudness = one(*cuts[0])
    for cut in cuts[1:]:
        loudness = loudness * one(*cut)
    return loudness


def normal_values(key, extent, deviation, most, cuts=(), kind=jnp.bfloat16):
    loudness = block_scale(key, extent, cuts, -0.22, 0.18) if cuts else 1.0
    result = jax.random.normal(key, extent, jnp.float32) * deviation * loudness
    return jnp.minimum(jnp.maximum(result, -most), most).astype(kind)


def setup_inputs(seed: int = 0) -> dict:
    splits = jax.random.split(jax.random.key(seed), 6)
    queries = draw_queries(jax.random.fold_in(splits[5], 71), 0)
    keys = draw_keys(jax.random.fold_in(splits[5], 71), 0)
    values = normal_values(splits[2], (TOKENS, D), 1.0, 6.0, ((0, 8), (1, 4)))
    cluster_ids = draw_cluster_ids(jax.random.fold_in(splits[5], 71), 0)
    out_weight = normal_values(splits[4], (D, D), HD ** -0.5, 0.5, ((0, 4),))
    return {"queries": queries, "keys": keys, "values": values, "cluster_ids": cluster_ids, "out_weight": out_weight}


def attend_block(query_rows, key_rows, value_rows, live_rows):
    scores = jnp.dot(query_rows, key_rows.T, preferred_element_type=jnp.float32) * (1.0 / math.sqrt(HD))
    order_index = jnp.arange(BLOCK, dtype=jnp.int32)
    before = order_index[None, :] <= order_index[:, None]
    itself = order_index[None, :] == order_index[:, None]
    allowed = before & ((live_rows[None, :] > 0) | itself)
    scores = jnp.where(allowed, scores, -1e+30)
    row_top = lax.optimization_barrier(jnp.max(scores, axis=1, keepdims=True))
    spread = jnp.exp(scores - row_top)
    weights = (spread / lax.optimization_barrier(jnp.sum(spread, axis=1, keepdims=True))).astype(jnp.bfloat16)
    return jnp.dot(weights, value_rows, preferred_element_type=jnp.float32).astype(jnp.bfloat16)

def reference(queries, keys, values, cluster_ids, out_weight):
    blocks = TOKENS // TOK_DEV
    total_rows = CLUSTERS * BLOCK

    def head_work(head):
        cluster_row = cluster_ids[head].reshape(blocks, TOK_DEV)
        position = jnp.arange(TOK_DEV, dtype=jnp.int32)
        earlier = position[None, :] < position[:, None]
        matching = cluster_row[:, :, None] == cluster_row[:, None, :]
        slot_rank = lax.optimization_barrier(jnp.sum((matching & earlier[None]).astype(jnp.int32), axis=2))
        block_index = jnp.arange(blocks, dtype=jnp.int32)[:, None]
        block_row = (cluster_row * BLOCK + block_index * MOST + slot_rank).reshape(TOKENS).astype(jnp.int32)
        start = (head * HD).astype(jnp.int32)
        query_head = lax.dynamic_slice_in_dim(queries, start, HD, 1)
        key_head = lax.dynamic_slice_in_dim(keys, start, HD, 1)
        value_head = lax.dynamic_slice_in_dim(values, start, HD, 1)
        query_pad = jnp.zeros((total_rows, HD), jnp.bfloat16).at[block_row].set(query_head)
        key_pad = jnp.zeros((total_rows, HD), jnp.bfloat16).at[block_row].set(key_head)
        value_pad = jnp.zeros((total_rows, HD), jnp.bfloat16).at[block_row].set(value_head)
        live_pad = jnp.zeros((total_rows,), jnp.int32).at[block_row].set(1)

        def cluster_work(cluster):
            first = (cluster * BLOCK).astype(jnp.int32)
            return attend_block(lax.dynamic_slice_in_dim(query_pad, first, BLOCK, 0), lax.dynamic_slice_in_dim(key_pad, first, BLOCK, 0), lax.dynamic_slice_in_dim(value_pad, first, BLOCK, 0), lax.dynamic_slice_in_dim(live_pad, first, BLOCK, 0))
        outputs = lax.map(cluster_work, jnp.arange(CLUSTERS, dtype=jnp.int32)).reshape(total_rows, HD)
        return outputs[block_row]
    attended = lax.map(head_work, jnp.arange(HEADS, dtype=jnp.int32))
    attended = jnp.transpose(attended, (1, 0, 2)).reshape(blocks, TOK_DEV, D)

    def project(rows):
        return jnp.dot(rows, out_weight, preferred_element_type=jnp.float32).astype(jnp.bfloat16)
    return lax.map(project, attended).reshape(TOKENS, D)
```

```python
import math

import jax
import jax.numpy as jnp
from jax import lax
from jax.experimental import pallas as pl
from jax.experimental.pallas import tpu as pltpu
from jax.sharding import PartitionSpec as P

CLUSTERS = 256
MOST = 4


def attend_block(query_part, key_part, value_part, filled_part, score_scale):
    owners, local_slots, head_width = query_part.shape
    local_count = filled_part.shape[1]
    slot_count = local_slots // local_count
    query_rows = query_part.reshape(owners, local_count, slot_count, head_width)
    key_rows = key_part.reshape(owners, local_count, slot_count, head_width)
    value_rows = value_part.reshape(owners, local_count, slot_count, head_width)
    scores = (
        jnp.einsum("scmd,tcnd->csmtn", query_rows, key_rows, preferred_element_type=jnp.float32)
        * score_scale
    )
    order_index = jnp.arange(owners * slot_count, dtype=jnp.int32).reshape(owners, slot_count)
    before = order_index[None, None, :, :] <= order_index[:, :, None, None]
    itself = order_index[None, None, :, :] == order_index[:, :, None, None]
    slot_value = jnp.arange(slot_count, dtype=jnp.float32)[None, None, :]
    taken_slot = slot_value < jnp.transpose(filled_part).astype(jnp.float32)[:, :, None]
    allowed = before[None] & (taken_slot[:, None, None, :, :] | itself[None])
    scores = jnp.where(allowed, scores, -1e30)
    row_top = jnp.max(scores, axis=(3, 4), keepdims=True)
    spread = jnp.exp(scores - row_top)
    weights = (spread / jnp.sum(spread, axis=(3, 4), keepdims=True)).astype(jnp.bfloat16)
    combined = jnp.einsum(
        "csmtn,tcnd->scmd", weights, value_rows, preferred_element_type=jnp.float32
    )
    return combined.astype(jnp.bfloat16).reshape(owners, local_slots, head_width)


def padded_plan(queries, keys, values, cluster_ids, out_weight):
    token_count = queries.shape[0]
    groups = cluster_ids.shape[0]
    head_width = queries.shape[1] // groups
    owners = lax.axis_size("seq")
    local_count = CLUSTERS // owners
    position = jnp.arange(token_count, dtype=jnp.int32)
    earlier = position[None, :] < position[:, None]
    matching = cluster_ids[:, :, None] == cluster_ids[:, None, :]
    slot_rank = jnp.sum((matching & earlier[None]).astype(jnp.int32), axis=2)
    owner_index = jnp.transpose(cluster_ids // local_count)
    within_owner = jnp.transpose(cluster_ids % local_count * MOST + slot_rank)
    head_index = jnp.arange(groups, dtype=jnp.int32)[None, :]

    def place(source):
        shaped = source.reshape(token_count, groups, head_width)
        blank = jnp.zeros((owners, groups, local_count * MOST, head_width), jnp.bfloat16)
        return blank.at[owner_index, head_index, within_owner].set(shaped)

    cluster_axis = jnp.arange(CLUSTERS, dtype=jnp.int32)
    filled = jnp.sum(
        (cluster_ids[:, :, None] == cluster_axis[None, None, :]).astype(jnp.int32), axis=1
    )
    filled = jnp.transpose(filled.reshape(groups, owners, local_count), (1, 0, 2)).astype(
        jnp.bfloat16
    )
    score_scale = 1.0 / math.sqrt(head_width)
    query_in = lax.all_to_all(place(queries), "seq", split_axis=0, concat_axis=0, tiled=True)
    key_in = lax.all_to_all(place(keys), "seq", split_axis=0, concat_axis=0, tiled=True)
    value_in = lax.all_to_all(place(values), "seq", split_axis=0, concat_axis=0, tiled=True)
    count_in = lax.all_to_all(filled, "seq", split_axis=0, concat_axis=0, tiled=True)

    def one_head(position_head):
        return attend_block(
            lax.dynamic_index_in_dim(query_in, position_head, 1, False),
            lax.dynamic_index_in_dim(key_in, position_head, 1, False),
            lax.dynamic_index_in_dim(value_in, position_head, 1, False),
            lax.dynamic_index_in_dim(count_in, position_head, 1, False),
            score_scale,
        )

    results = lax.map(one_head, jnp.arange(query_in.shape[1], dtype=jnp.int32))
    returned = lax.all_to_all(results, "seq", split_axis=1, concat_axis=1, tiled=True)
    gathered = returned[head_index, owner_index, within_owner]
    attended = gathered.reshape(token_count, groups * head_width)
    partial_sums = jnp.dot(attended, out_weight, preferred_element_type=jnp.float32)
    summed = lax.psum_scatter(partial_sums, "head", scatter_dimension=1, tiled=True)
    return summed.astype(jnp.bfloat16)


ID_ROWS = 16
MISMATCH = 262144.0


def pack_kernel(place_ref, q_ref, k_ref, v_ref, ids_ref, *outs):
    heads = ids_ref.shape[0]
    rows, width = outs[0].shape
    parts = rows // width
    for offset in range(heads):
        q_out, kv_out = outs[2 * offset], outs[2 * offset + 1]
        head = lax.bitwise_xor(place_ref[0], offset)
        columns = pl.ds(pl.multiple_of(head * width, width), width)
        kv_out[pl.ds(0, rows), :] = k_ref[:, columns]
        kv_out[pl.ds(rows, rows), :] = v_ref[:, columns]
        q_out[...] = q_ref[:, columns]
        ids = ids_ref[pl.ds(head, 1), :].astype(jnp.float32)
        lines = [ids[:, part * width : (part + 1) * width] for part in range(parts)]
        lines.append(jnp.zeros((ID_ROWS - parts, width), jnp.float32))
        kv_out[pl.ds(2 * rows, ID_ROWS), :] = jnp.concatenate(lines, axis=0).astype(jnp.bfloat16)


def pack(place, queries, keys, values, cluster_ids):
    heads = cluster_ids.shape[0]
    rows = queries.shape[0]
    width = queries.shape[1] // heads
    local_memory = pl.BlockSpec(memory_space=pltpu.VMEM)
    pair = [
        jax.ShapeDtypeStruct((rows, width), jnp.bfloat16),
        jax.ShapeDtypeStruct((2 * rows + ID_ROWS, width), jnp.bfloat16),
    ]
    outs = pl.pallas_call(
        pack_kernel,
        out_shape=tuple(pair * heads),
        in_specs=[pl.BlockSpec(memory_space=pltpu.SMEM)] + [local_memory] * 4,
        out_specs=(local_memory,) * (2 * heads),
        name="pack",
    )(place, queries, keys, values, cluster_ids)
    return outs[0::2], outs[1::2]


def attend_kernel(scale, where_ref, *refs):
    pieces = (len(refs) - 6) // 4
    own_refs, far_refs, q_refs, out_refs = (refs[pieces * kind : pieces * (kind + 1)] for kind in range(4))
    k_all, v_all, q_all, ids_all, out_all, sems = refs[4 * pieces :]
    rows, width = q_refs[0].shape
    parts = rows // width
    tile = 256
    started = []
    slots = [lax.bitwise_xor(where_ref[0], offset) for offset in range(pieces)]
    spans = [pl.ds(pl.multiple_of(slot * rows, rows), rows) for slot in slots]

    def fetch(source, target):
        copy = pltpu.make_async_copy(source, target, sems.at[len(started)])
        copy.start()
        started.append(copy)

    for side, side_refs in enumerate((own_refs, far_refs)):
        for ref, slot in zip(side_refs, slots):
            fetch(ref.at[pl.ds(2 * rows, ID_ROWS)], ids_all.at[side, slot])
    for ref, span in zip(q_refs, spans):
        fetch(ref, q_all.at[span, pl.ds(0, width)])
    for side, side_refs in enumerate((own_refs, far_refs)):
        for ref, span in zip(side_refs, spans):
            fetch(ref.at[pl.ds(0, rows)], k_all.at[side, span, pl.ds(0, width)])
            fetch(ref.at[pl.ds(rows, rows)], v_all.at[side, span, pl.ds(0, width)])
    v_all[:, :, width:] = jnp.ones((2, pieces * rows, width), jnp.bfloat16)
    for copy in started[: 2 * pieces]:
        copy.wait()
    lane = lax.broadcasted_iota(jnp.int32, (width, width), 1)
    shift = jnp.minimum(lane // 2, 8)
    odd = lane % 2
    live = lane < 16
    for side in range(2):
        for piece in range(pieces):
            ids = ids_all[side, piece].astype(jnp.float32)
            for part in range(parts):
                line = jnp.broadcast_to(ids[part : part + 1], (width, width)).T.astype(jnp.int32)
                flag = lax.bitwise_xor(lax.bitwise_and(lax.shift_right_logical(line, shift), 1), odd)
                here = pl.ds(piece * rows + part * width, width)
                mark = jnp.where(live, flag.astype(jnp.float32), 0.0)
                k_all[side, here, width:] = mark.astype(jnp.bfloat16)
                if side == 0:
                    other = jnp.where(live, (flag.astype(jnp.float32) - 1.0) * MISMATCH, 0.0)
                    q_all[here, width:] = other.astype(jnp.bfloat16)
    for copy in started[2 * pieces :]:
        copy.wait()

    later = where_ref[1]
    far_bias = jnp.where(later > 0, 0.0, -MISMATCH * 4.0).astype(jnp.float32)
    factor = scale * math.log2(math.e)
    contract = (((1,), (1,)), ((), ()))
    for piece in range(pieces):
        span = (piece + 1) * rows
        for step in range(rows // tile):
            q = q_all[pl.ds(piece * rows + step * tile, tile), :]
            own = lax.dot_general(q, k_all[0, pl.ds(0, span), :], contract, preferred_element_type=jnp.float32)
            far = lax.dot_general(q, k_all[1, pl.ds(0, span), :], contract, preferred_element_type=jnp.float32)
            before = piece * rows
            row = lax.broadcasted_iota(jnp.int32, (tile, rows), 0) + step * tile
            column = lax.broadcasted_iota(jnp.int32, (tile, rows), 1)
            diagonal = jnp.where(column <= row, own[:, before:], -MISMATCH * 4.0)
            last = far[:, before:] + far_bias
            if piece:
                own = jnp.concatenate([own[:, :before], diagonal], axis=1)
                far = jnp.concatenate([far[:, :before], last], axis=1)
            else:
                own, far = diagonal, last
            top = jnp.maximum(own[:, :width], far[:, :width])
            for start in range(width, span, width):
                top = jnp.maximum(top, own[:, start : start + width])
                top = jnp.maximum(top, far[:, start : start + width])
            top = jnp.max(top, axis=1, keepdims=True) * factor
            own = jnp.exp2(own * factor - top).astype(jnp.bfloat16)
            far = jnp.exp2(far * factor - top).astype(jnp.bfloat16)
            total = jnp.dot(own, v_all[0, pl.ds(0, span), :], preferred_element_type=jnp.float32)
            total = total + jnp.dot(far, v_all[1, pl.ds(0, span), :], preferred_element_type=jnp.float32)
            result = total[:, :width] / total[:, width:]
            out_all[piece, pl.ds(step * tile, tile), :] = result.astype(jnp.bfloat16)
    started.clear()
    for ref, slot in zip(out_refs, slots):
        fetch(out_all.at[slot], ref)
    for copy in started:
        copy.wait()


def attend(where, kv_own, kv_far, q):
    pieces = len(q)
    rows, width = q[0].shape
    anywhere = pl.BlockSpec(memory_space=pl.ANY)
    return pl.pallas_call(
        lambda *refs: attend_kernel(1.0 / math.sqrt(width), *refs),
        out_shape=(jax.ShapeDtypeStruct((rows, width), jnp.bfloat16),) * pieces,
        in_specs=[pl.BlockSpec(memory_space=pltpu.SMEM)] + [anywhere] * (3 * pieces),
        out_specs=(anywhere,) * pieces,
        scratch_shapes=[
            pltpu.VMEM((2, pieces * rows, 2 * width), jnp.bfloat16),
            pltpu.VMEM((2, pieces * rows, 2 * width), jnp.bfloat16),
            pltpu.VMEM((pieces * rows, 2 * width), jnp.bfloat16),
            pltpu.VMEM((2, pieces, ID_ROWS, width), jnp.bfloat16),
            pltpu.VMEM((pieces, rows, width), jnp.bfloat16),
            pltpu.SemaphoreType.DMA((7 * pieces,)),
        ],
        compiler_params=pltpu.CompilerParams(vmem_limit_bytes=48 * 1024 * 1024),
        name="attend",
    )(where, *kv_own, *kv_far, *q)


def project_kernel(where_ref, *refs):
    pieces = (len(refs) - 8) // 4
    a_refs, w_refs = refs[: 4 * pieces], refs[4 * pieces : 4 * pieces + 4]
    out_ref, a_all, w_all, sems = refs[4 * pieces + 4 :]
    rows, width = a_refs[0].shape
    place, here = where_ref[0], where_ref[2]
    started = []

    def fetch(source, target):
        copy = pltpu.make_async_copy(source, target, sems.at[len(started)])
        copy.start()
        started.append(copy)

    for far in range(4):
        group = lax.bitwise_xor(here, far)
        fetch(w_refs[far], w_all.at[group])
        for offset in range(pieces):
            head = lax.bitwise_xor(place, offset)
            columns = pl.ds(pl.multiple_of(head * width, width), width)
            fetch(a_refs[far * pieces + offset], a_all.at[group, :, columns])
    for copy in started:
        copy.wait()
    total = jnp.dot(a_all[0], w_all[0], preferred_element_type=jnp.float32)
    for group in range(1, 4):
        total = total + jnp.dot(a_all[group], w_all[group], preferred_element_type=jnp.float32)
    out_ref[...] = total.astype(jnp.bfloat16)


def project(where, blocks, weights):
    pieces = len(blocks[0])
    rows, width = blocks[0][0].shape
    anywhere = pl.BlockSpec(memory_space=pl.ANY)
    return pl.pallas_call(
        project_kernel,
        out_shape=jax.ShapeDtypeStruct((rows, weights[0].shape[1]), jnp.bfloat16),
        in_specs=[pl.BlockSpec(memory_space=pltpu.SMEM)] + [anywhere] * (4 * pieces + 4),
        out_specs=pl.BlockSpec(memory_space=pltpu.VMEM),
        scratch_shapes=[
            pltpu.VMEM((4, rows, pieces * width), jnp.bfloat16),
            pltpu.VMEM((4,) + weights[0].shape, jnp.bfloat16),
            pltpu.SemaphoreType.DMA((4 + 4 * pieces,)),
        ],
        compiler_params=pltpu.CompilerParams(vmem_limit_bytes=32 * 1024 * 1024),
        name="project",
    )(where, *[piece for block in blocks for piece in block], *weights)


def head_plan(queries, keys, values, cluster_ids, out_weight):
    heads = cluster_ids.shape[0]
    seq = lax.axis_index("seq").astype(jnp.int32)
    here = lax.axis_index("head").astype(jnp.int32)
    where = jnp.stack([seq // 2, seq % 2, here])

    def swap(array, axis, bits):
        size = lax.axis_size(axis)
        return lax.ppermute(array, axis, [(place, place ^ bits) for place in range(size)])

    def after(array, *others):
        return lax.optimization_barrier((array,) + others)[0]

    q, kv = pack(where, queries, keys, values, cluster_ids)
    kv_own, kv_far, q_own = [kv[0]] + [None] * 3, [None] * 4, [q[0]] + [None] * 3
    for offset in (2, 3, 1):
        kv_own[offset] = swap(kv[offset], "seq", 2 * offset)
    kv_far[0] = swap(kv[0], "seq", 1)
    columns = out_weight.shape[1] // 4
    weights = []
    late_weight = after(out_weight, kv[1])
    for far in range(4):
        block = lax.dynamic_slice_in_dim(late_weight, (here ^ far) * columns, columns, 1)
        weights.append(swap(block, "head", far) if far else block)
    for offset in (1, 2, 3):
        kv_far[offset] = swap(kv_own[offset], "seq", 1)
    for offset in (2, 3, 1):
        q_own[offset] = swap(after(q[offset], kv_own[2], kv_own[3]), "seq", 2 * offset)
    attended = list(attend(where, kv_own, kv_far, q_own))
    for offset in range(1, heads):
        attended[offset] = swap(attended[offset], "seq", 2 * offset)
    across = [swap(piece, "head", 2) for piece in attended]
    blocks = [attended, [swap(piece, "head", 1) for piece in attended], across, [swap(piece, "head", 1) for piece in across]]
    return project(where, blocks, weights)


def local(queries, keys, values, cluster_ids, out_weight):
    groups = cluster_ids.shape[0]
    if lax.axis_size("seq") == 2 * groups and lax.axis_size("head") == 4:
        return head_plan(queries, keys, values, cluster_ids, out_weight)
    return padded_plan(queries, keys, values, cluster_ids, out_weight)


def solution(mesh):
    placed = (
        P("seq", "head"),
        P("seq", "head"),
        P("seq", "head"),
        P("head", "seq"),
        P("head", None),
    )
    return jax.shard_map(
        local, mesh=mesh, in_specs=placed, out_specs=P("seq", "head"), check_vma=False
    )
```

```python
import math

import jax
import jax.numpy as jnp
from jax import lax
from jax.experimental import pallas as pl
from jax.experimental.pallas import tpu as pltpu
from jax.sharding import PartitionSpec as P

CLUSTERS = 256
MOST = 4


def attend_block(query_part, key_part, value_part, filled_part, score_scale):
    owners, local_slots, head_width = query_part.shape
    local_count = filled_part.shape[1]
    slot_count = local_slots // local_count
    query_rows = query_part.reshape(owners, local_count, slot_count, head_width)
    key_rows = key_part.reshape(owners, local_count, slot_count, head_width)
    value_rows = value_part.reshape(owners, local_count, slot_count, head_width)
    scores = (
        jnp.einsum("scmd,tcnd->csmtn", query_rows, key_rows, preferred_element_type=jnp.float32)
        * score_scale
    )
    order_index = jnp.arange(owners * slot_count, dtype=jnp.int32).reshape(owners, slot_count)
    before = order_index[None, None, :, :] <= order_index[:, :, None, None]
    itself = order_index[None, None, :, :] == order_index[:, :, None, None]
    slot_value = jnp.arange(slot_count, dtype=jnp.float32)[None, None, :]
    taken_slot = slot_value < jnp.transpose(filled_part).astype(jnp.float32)[:, :, None]
    allowed = before[None] & (taken_slot[:, None, None, :, :] | itself[None])
    scores = jnp.where(allowed, scores, -1e30)
    row_top = jnp.max(scores, axis=(3, 4), keepdims=True)
    spread = jnp.exp(scores - row_top)
    weights = (spread / jnp.sum(spread, axis=(3, 4), keepdims=True)).astype(jnp.bfloat16)
    combined = jnp.einsum(
        "csmtn,tcnd->scmd", weights, value_rows, preferred_element_type=jnp.float32
    )
    return combined.astype(jnp.bfloat16).reshape(owners, local_slots, head_width)


def padded_plan(queries, keys, values, cluster_ids, out_weight):
    token_count = queries.shape[0]
    groups = cluster_ids.shape[0]
    head_width = queries.shape[1] // groups
    owners = lax.axis_size("seq")
    local_count = CLUSTERS // owners
    position = jnp.arange(token_count, dtype=jnp.int32)
    earlier = position[None, :] < position[:, None]
    matching = cluster_ids[:, :, None] == cluster_ids[:, None, :]
    slot_rank = jnp.sum((matching & earlier[None]).astype(jnp.int32), axis=2)
    owner_index = jnp.transpose(cluster_ids // local_count)
    within_owner = jnp.transpose(cluster_ids % local_count * MOST + slot_rank)
    head_index = jnp.arange(groups, dtype=jnp.int32)[None, :]

    def place(source):
        shaped = source.reshape(token_count, groups, head_width)
        blank = jnp.zeros((owners, groups, local_count * MOST, head_width), jnp.bfloat16)
        return blank.at[owner_index, head_index, within_owner].set(shaped)

    cluster_axis = jnp.arange(CLUSTERS, dtype=jnp.int32)
    filled = jnp.sum(
        (cluster_ids[:, :, None] == cluster_axis[None, None, :]).astype(jnp.int32), axis=1
    )
    filled = jnp.transpose(filled.reshape(groups, owners, local_count), (1, 0, 2)).astype(
        jnp.bfloat16
    )
    score_scale = 1.0 / math.sqrt(head_width)
    query_in = lax.all_to_all(place(queries), "seq", split_axis=0, concat_axis=0, tiled=True)
    key_in = lax.all_to_all(place(keys), "seq", split_axis=0, concat_axis=0, tiled=True)
    value_in = lax.all_to_all(place(values), "seq", split_axis=0, concat_axis=0, tiled=True)
    count_in = lax.all_to_all(filled, "seq", split_axis=0, concat_axis=0, tiled=True)

    def one_head(position_head):
        return attend_block(
            lax.dynamic_index_in_dim(query_in, position_head, 1, False),
            lax.dynamic_index_in_dim(key_in, position_head, 1, False),
            lax.dynamic_index_in_dim(value_in, position_head, 1, False),
            lax.dynamic_index_in_dim(count_in, position_head, 1, False),
            score_scale,
        )

    results = lax.map(one_head, jnp.arange(query_in.shape[1], dtype=jnp.int32))
    returned = lax.all_to_all(results, "seq", split_axis=1, concat_axis=1, tiled=True)
    gathered = returned[head_index, owner_index, within_owner]
    attended = gathered.reshape(token_count, groups * head_width)
    partial_sums = jnp.dot(attended, out_weight, preferred_element_type=jnp.float32)
    summed = lax.psum_scatter(partial_sums, "head", scatter_dimension=1, tiled=True)
    return summed.astype(jnp.bfloat16)


ID_ROWS = 16
MISMATCH = 262144.0


def pack_kernel(place_ref, q_ref, k_ref, v_ref, ids_ref, *outs):
    heads = ids_ref.shape[0]
    rows, width = outs[0].shape
    parts = rows // width
    for offset in range(heads):
        q_out, kv_out = outs[2 * offset], outs[2 * offset + 1]
        head = lax.bitwise_xor(place_ref[0], offset)
        columns = pl.ds(pl.multiple_of(head * width, width), width)
        kv_out[pl.ds(0, rows), :] = k_ref[:, columns]
        kv_out[pl.ds(rows, rows), :] = v_ref[:, columns]
        q_out[...] = q_ref[:, columns]
        ids = ids_ref[pl.ds(head, 1), :].astype(jnp.float32)
        lines = [ids[:, part * width : (part + 1) * width] for part in range(parts)]
        lines.append(jnp.zeros((ID_ROWS - parts, width), jnp.float32))
        kv_out[pl.ds(2 * rows, ID_ROWS), :] = jnp.concatenate(lines, axis=0).astype(jnp.bfloat16)


def pack(place, queries, keys, values, cluster_ids):
    heads = cluster_ids.shape[0]
    rows = queries.shape[0]
    width = queries.shape[1] // heads
    local_memory = pl.BlockSpec(memory_space=pltpu.VMEM)
    pair = [
        jax.ShapeDtypeStruct((rows, width), jnp.bfloat16),
        jax.ShapeDtypeStruct((2 * rows + ID_ROWS, width), jnp.bfloat16),
    ]
    outs = pl.pallas_call(
        pack_kernel,
        out_shape=tuple(pair * heads),
        in_specs=[pl.BlockSpec(memory_space=pltpu.SMEM)] + [local_memory] * 4,
        out_specs=(local_memory,) * (2 * heads),
        name="pack",
    )(place, queries, keys, values, cluster_ids)
    return outs[0::2], outs[1::2]


def attend_kernel(scale, where_ref, *refs):
    pieces = (len(refs) - 6) // 4
    own_refs, far_refs, q_refs, out_refs = (refs[pieces * kind : pieces * (kind + 1)] for kind in range(4))
    k_all, v_all, q_all, ids_all, out_all, sems = refs[4 * pieces :]
    rows, width = q_refs[0].shape
    parts = rows // width
    tile = 256
    started = []
    slots = [lax.bitwise_xor(where_ref[0], offset) for offset in range(pieces)]
    spans = [pl.ds(pl.multiple_of(slot * rows, rows), rows) for slot in slots]

    def fetch(source, target):
        copy = pltpu.make_async_copy(source, target, sems.at[len(started)])
        copy.start()
        started.append(copy)

    for side, side_refs in enumerate((own_refs, far_refs)):
        for ref, slot in zip(side_refs, slots):
            fetch(ref.at[pl.ds(2 * rows, ID_ROWS)], ids_all.at[side, slot])
    for ref, span in zip(q_refs, spans):
        fetch(ref, q_all.at[span, pl.ds(0, width)])
    for side, side_refs in enumerate((own_refs, far_refs)):
        for ref, span in zip(side_refs, spans):
            fetch(ref.at[pl.ds(0, rows)], k_all.at[side, span, pl.ds(0, width)])
            fetch(ref.at[pl.ds(rows, rows)], v_all.at[side, span, pl.ds(0, width)])
    v_all[:, :, width:] = jnp.ones((2, pieces * rows, width), jnp.bfloat16)
    for copy in started[: 2 * pieces]:
        copy.wait()
    lane = lax.broadcasted_iota(jnp.int32, (width, width), 1)
    shift = jnp.minimum(lane // 2, 8)
    odd = lane % 2
    live = lane < 16
    for side in range(2):
        for piece in range(pieces):
            ids = ids_all[side, piece].astype(jnp.float32)
            for part in range(parts):
                line = jnp.broadcast_to(ids[part : part + 1], (width, width)).T.astype(jnp.int32)
                flag = lax.bitwise_xor(lax.bitwise_and(lax.shift_right_logical(line, shift), 1), odd)
                here = pl.ds(piece * rows + part * width, width)
                mark = jnp.where(live, flag.astype(jnp.float32), 0.0)
                k_all[side, here, width:] = mark.astype(jnp.bfloat16)
                if side == 0:
                    other = jnp.where(live, (flag.astype(jnp.float32) - 1.0) * MISMATCH, 0.0)
                    q_all[here, width:] = other.astype(jnp.bfloat16)
    for copy in started[2 * pieces :]:
        copy.wait()

    later = where_ref[1]
    far_bias = jnp.where(later > 0, 0.0, -MISMATCH * 4.0).astype(jnp.float32)
    factor = scale * math.log2(math.e)
    contract = (((1,), (1,)), ((), ()))
    for piece in range(pieces):
        span = (piece + 1) * rows
        for step in range(rows // tile):
            q = q_all[pl.ds(piece * rows + step * tile, tile), :]
            own = lax.dot_general(q, k_all[0, pl.ds(0, span), :], contract, preferred_element_type=jnp.float32)
            far = lax.dot_general(q, k_all[1, pl.ds(0, span), :], contract, preferred_element_type=jnp.float32)
            before = piece * rows
            row = lax.broadcasted_iota(jnp.int32, (tile, rows), 0) + step * tile
            column = lax.broadcasted_iota(jnp.int32, (tile, rows), 1)
            diagonal = jnp.where(column <= row, own[:, before:], -MISMATCH * 4.0)
            last = far[:, before:] + far_bias
            if piece:
                own = jnp.concatenate([own[:, :before], diagonal], axis=1)
                far = jnp.concatenate([far[:, :before], last], axis=1)
            else:
                own, far = diagonal, last
            top = jnp.maximum(own[:, :width], far[:, :width])
            for start in range(width, span, width):
                top = jnp.maximum(top, own[:, start : start + width])
                top = jnp.maximum(top, far[:, start : start + width])
            top = jnp.max(top, axis=1, keepdims=True) * factor
            own = jnp.exp2(own * factor - top).astype(jnp.bfloat16)
            far = jnp.exp2(far * factor - top).astype(jnp.bfloat16)
            total = jnp.dot(own, v_all[0, pl.ds(0, span), :], preferred_element_type=jnp.float32)
            total = total + jnp.dot(far, v_all[1, pl.ds(0, span), :], preferred_element_type=jnp.float32)
            result = total[:, :width] / total[:, width:]
            out_all[piece, pl.ds(step * tile, tile), :] = result.astype(jnp.bfloat16)
    started.clear()
    for ref, slot in zip(out_refs, slots):
        fetch(out_all.at[slot], ref)
    for copy in started:
        copy.wait()


def attend(where, kv_own, kv_far, q):
    pieces = len(q)
    rows, width = q[0].shape
    anywhere = pl.BlockSpec(memory_space=pl.ANY)
    return pl.pallas_call(
        lambda *refs: attend_kernel(1.0 / math.sqrt(width), *refs),
        out_shape=(jax.ShapeDtypeStruct((rows, width), jnp.bfloat16),) * pieces,
        in_specs=[pl.BlockSpec(memory_space=pltpu.SMEM)] + [anywhere] * (3 * pieces),
        out_specs=(anywhere,) * pieces,
        scratch_shapes=[
            pltpu.VMEM((2, pieces * rows, 2 * width), jnp.bfloat16),
            pltpu.VMEM((2, pieces * rows, 2 * width), jnp.bfloat16),
            pltpu.VMEM((pieces * rows, 2 * width), jnp.bfloat16),
            pltpu.VMEM((2, pieces, ID_ROWS, width), jnp.bfloat16),
            pltpu.VMEM((pieces, rows, width), jnp.bfloat16),
            pltpu.SemaphoreType.DMA((7 * pieces,)),
        ],
        compiler_params=pltpu.CompilerParams(vmem_limit_bytes=48 * 1024 * 1024),
        name="attend",
    )(where, *kv_own, *kv_far, *q)


def project_kernel(where_ref, *refs):
    pieces = (len(refs) - 8) // 4
    a_refs, w_refs = refs[: 4 * pieces], refs[4 * pieces : 4 * pieces + 4]
    out_ref, a_all, w_all, sems = refs[4 * pieces + 4 :]
    rows, width = a_refs[0].shape
    place, here = where_ref[0], where_ref[2]
    started = []

    def fetch(source, target):
        copy = pltpu.make_async_copy(source, target, sems.at[len(started)])
        copy.start()
        started.append(copy)

    for far in range(4):
        group = lax.bitwise_xor(here, far)
        fetch(w_refs[far], w_all.at[group])
        for offset in range(pieces):
            head = lax.bitwise_xor(place, offset)
            columns = pl.ds(pl.multiple_of(head * width, width), width)
            fetch(a_refs[far * pieces + offset], a_all.at[group, :, columns])
    for copy in started:
        copy.wait()
    total = jnp.dot(a_all[0], w_all[0], preferred_element_type=jnp.float32)
    for group in range(1, 4):
        total = total + jnp.dot(a_all[group], w_all[group], preferred_element_type=jnp.float32)
    out_ref[...] = total.astype(jnp.bfloat16)


def project(where, blocks, weights):
    pieces = len(blocks[0])
    rows, width = blocks[0][0].shape
    anywhere = pl.BlockSpec(memory_space=pl.ANY)
    return pl.pallas_call(
        project_kernel,
        out_shape=jax.ShapeDtypeStruct((rows, weights[0].shape[1]), jnp.bfloat16),
        in_specs=[pl.BlockSpec(memory_space=pltpu.SMEM)] + [anywhere] * (4 * pieces + 4),
        out_specs=pl.BlockSpec(memory_space=pltpu.VMEM),
        scratch_shapes=[
            pltpu.VMEM((4, rows, pieces * width), jnp.bfloat16),
            pltpu.VMEM((4,) + weights[0].shape, jnp.bfloat16),
            pltpu.SemaphoreType.DMA((4 + 4 * pieces,)),
        ],
        compiler_params=pltpu.CompilerParams(vmem_limit_bytes=32 * 1024 * 1024),
        name="project",
    )(where, *[piece for block in blocks for piece in block], *weights)


def head_plan(queries, keys, values, cluster_ids, out_weight):
    heads = cluster_ids.shape[0]
    seq = lax.axis_index("seq").astype(jnp.int32)
    here = lax.axis_index("head").astype(jnp.int32)
    where = jnp.stack([seq // 2, seq % 2, here])

    def swap(array, axis, bits):
        size = lax.axis_size(axis)
        return lax.ppermute(array, axis, [(place, place ^ bits) for place in range(size)])

    def after(array, *others):
        return lax.optimization_barrier((array,) + others)[0]

    q, kv = pack(where, queries, keys, values, cluster_ids)
    kv_own, kv_far, q_own = [kv[0]] + [None] * 3, [None] * 4, [q[0]] + [None] * 3
    kv_own[2] = swap(kv[2], "seq", 4)
    kv_own[1] = swap(kv[1], "seq", 2)
    kv_far[0] = swap(kv[0], "seq", 1)
    kv_own[3] = swap(after(kv[3], kv_own[1]), "seq", 6)
    columns = out_weight.shape[1] // 4
    weights = []
    late_weight = after(out_weight, kv[1])
    for far in range(4):
        block = lax.dynamic_slice_in_dim(late_weight, (here ^ far) * columns, columns, 1)
        weights.append(swap(block, "head", far) if far else block)
    for offset in (1, 2, 3):
        kv_far[offset] = swap(kv_own[offset], "seq", 1)
    q_own[2] = swap(after(q[2], kv_own[2]), "seq", 4)
    for offset in (3, 1):
        q_own[offset] = swap(after(q[offset], kv_own[3]), "seq", 2 * offset)
    attended = list(attend(where, kv_own, kv_far, q_own))
    for offset in range(1, heads):
        attended[offset] = swap(attended[offset], "seq", 2 * offset)
    across = [swap(piece, "head", 2) for piece in attended]
    blocks = [attended, [swap(piece, "head", 1) for piece in attended], across, [swap(piece, "head", 1) for piece in across]]
    return project(where, blocks, weights)


def local(queries, keys, values, cluster_ids, out_weight):
    groups = cluster_ids.shape[0]
    if lax.axis_size("seq") == 2 * groups and lax.axis_size("head") == 4:
        return head_plan(queries, keys, values, cluster_ids, out_weight)
    return padded_plan(queries, keys, values, cluster_ids, out_weight)


def solution(mesh):
    placed = (
        P("seq", "head"),
        P("seq", "head"),
        P("seq", "head"),
        P("head", "seq"),
        P("head", None),
    )
    return jax.shard_map(
        local, mesh=mesh, in_specs=placed, out_specs=P("seq", "head"), check_vma=False
    )
```

```python
import math

import jax
import jax.numpy as jnp
from jax import lax
from jax.experimental import pallas as pl
from jax.experimental.pallas import tpu as pltpu
from jax.sharding import PartitionSpec as P

CLUSTERS = 256
MOST = 4


def attend_block(query_part, key_part, value_part, filled_part, score_scale):
    owners, local_slots, head_width = query_part.shape
    local_count = filled_part.shape[1]
    slot_count = local_slots // local_count
    query_rows = query_part.reshape(owners, local_count, slot_count, head_width)
    key_rows = key_part.reshape(owners, local_count, slot_count, head_width)
    value_rows = value_part.reshape(owners, local_count, slot_count, head_width)
    scores = (
        jnp.einsum("scmd,tcnd->csmtn", query_rows, key_rows, preferred_element_type=jnp.float32)
        * score_scale
    )
    order_index = jnp.arange(owners * slot_count, dtype=jnp.int32).reshape(owners, slot_count)
    before = order_index[None, None, :, :] <= order_index[:, :, None, None]
    itself = order_index[None, None, :, :] == order_index[:, :, None, None]
    slot_value = jnp.arange(slot_count, dtype=jnp.float32)[None, None, :]
    taken_slot = slot_value < jnp.transpose(filled_part).astype(jnp.float32)[:, :, None]
    allowed = before[None] & (taken_slot[:, None, None, :, :] | itself[None])
    scores = jnp.where(allowed, scores, -1e30)
    row_top = jnp.max(scores, axis=(3, 4), keepdims=True)
    spread = jnp.exp(scores - row_top)
    weights = (spread / jnp.sum(spread, axis=(3, 4), keepdims=True)).astype(jnp.bfloat16)
    combined = jnp.einsum(
        "csmtn,tcnd->scmd", weights, value_rows, preferred_element_type=jnp.float32
    )
    return combined.astype(jnp.bfloat16).reshape(owners, local_slots, head_width)


def padded_plan(queries, keys, values, cluster_ids, out_weight):
    token_count = queries.shape[0]
    groups = cluster_ids.shape[0]
    head_width = queries.shape[1] // groups
    owners = lax.axis_size("seq")
    local_count = CLUSTERS // owners
    position = jnp.arange(token_count, dtype=jnp.int32)
    earlier = position[None, :] < position[:, None]
    matching = cluster_ids[:, :, None] == cluster_ids[:, None, :]
    slot_rank = jnp.sum((matching & earlier[None]).astype(jnp.int32), axis=2)
    owner_index = jnp.transpose(cluster_ids // local_count)
    within_owner = jnp.transpose(cluster_ids % local_count * MOST + slot_rank)
    head_index = jnp.arange(groups, dtype=jnp.int32)[None, :]

    def place(source):
        shaped = source.reshape(token_count, groups, head_width)
        blank = jnp.zeros((owners, groups, local_count * MOST, head_width), jnp.bfloat16)
        return blank.at[owner_index, head_index, within_owner].set(shaped)

    cluster_axis = jnp.arange(CLUSTERS, dtype=jnp.int32)
    filled = jnp.sum(
        (cluster_ids[:, :, None] == cluster_axis[None, None, :]).astype(jnp.int32), axis=1
    )
    filled = jnp.transpose(filled.reshape(groups, owners, local_count), (1, 0, 2)).astype(
        jnp.bfloat16
    )
    score_scale = 1.0 / math.sqrt(head_width)
    query_in = lax.all_to_all(place(queries), "seq", split_axis=0, concat_axis=0, tiled=True)
    key_in = lax.all_to_all(place(keys), "seq", split_axis=0, concat_axis=0, tiled=True)
    value_in = lax.all_to_all(place(values), "seq", split_axis=0, concat_axis=0, tiled=True)
    count_in = lax.all_to_all(filled, "seq", split_axis=0, concat_axis=0, tiled=True)

    def one_head(position_head):
        return attend_block(
            lax.dynamic_index_in_dim(query_in, position_head, 1, False),
            lax.dynamic_index_in_dim(key_in, position_head, 1, False),
            lax.dynamic_index_in_dim(value_in, position_head, 1, False),
            lax.dynamic_index_in_dim(count_in, position_head, 1, False),
            score_scale,
        )

    results = lax.map(one_head, jnp.arange(query_in.shape[1], dtype=jnp.int32))
    returned = lax.all_to_all(results, "seq", split_axis=1, concat_axis=1, tiled=True)
    gathered = returned[head_index, owner_index, within_owner]
    attended = gathered.reshape(token_count, groups * head_width)
    partial_sums = jnp.dot(attended, out_weight, preferred_element_type=jnp.float32)
    summed = lax.psum_scatter(partial_sums, "head", scatter_dimension=1, tiled=True)
    return summed.astype(jnp.bfloat16)


ID_ROWS = 16
MISMATCH = 262144.0


def pack_kernel(place_ref, q_ref, k_ref, v_ref, ids_ref, *outs):
    heads = ids_ref.shape[0]
    rows, width = outs[0].shape
    parts = rows // width
    for offset in range(heads):
        q_out, kv_out = outs[2 * offset], outs[2 * offset + 1]
        head = lax.bitwise_xor(place_ref[0], offset)
        columns = pl.ds(pl.multiple_of(head * width, width), width)
        kv_out[pl.ds(0, rows), :] = k_ref[:, columns]
        kv_out[pl.ds(rows, rows), :] = v_ref[:, columns]
        q_out[...] = q_ref[:, columns]
        ids = ids_ref[pl.ds(head, 1), :].astype(jnp.float32)
        lines = [ids[:, part * width : (part + 1) * width] for part in range(parts)]
        lines.append(jnp.zeros((ID_ROWS - parts, width), jnp.float32))
        kv_out[pl.ds(2 * rows, ID_ROWS), :] = jnp.concatenate(lines, axis=0).astype(jnp.bfloat16)


def pack(place, queries, keys, values, cluster_ids):
    heads = cluster_ids.shape[0]
    rows = queries.shape[0]
    width = queries.shape[1] // heads
    local_memory = pl.BlockSpec(memory_space=pltpu.VMEM)
    pair = [
        jax.ShapeDtypeStruct((rows, width), jnp.bfloat16),
        jax.ShapeDtypeStruct((2 * rows + ID_ROWS, width), jnp.bfloat16),
    ]
    outs = pl.pallas_call(
        pack_kernel,
        out_shape=tuple(pair * heads),
        in_specs=[pl.BlockSpec(memory_space=pltpu.SMEM)] + [local_memory] * 4,
        out_specs=(local_memory,) * (2 * heads),
        name="pack",
    )(place, queries, keys, values, cluster_ids)
    return outs[0::2], outs[1::2]


def attend_kernel(scale, where_ref, *refs):
    pieces = (len(refs) - 6) // 4
    own_refs, far_refs, q_refs, out_refs = (refs[pieces * kind : pieces * (kind + 1)] for kind in range(4))
    k_all, v_all, q_all, ids_all, out_all, sems = refs[4 * pieces :]
    rows, width = q_refs[0].shape
    parts = rows // width
    tile = 256
    started = []
    slots = [lax.bitwise_xor(where_ref[0], offset) for offset in range(pieces)]
    spans = [pl.ds(pl.multiple_of(slot * rows, rows), rows) for slot in slots]

    def fetch(source, target):
        copy = pltpu.make_async_copy(source, target, sems.at[len(started)])
        copy.start()
        started.append(copy)

    for side, side_refs in enumerate((own_refs, far_refs)):
        for ref, slot in zip(side_refs, slots):
            fetch(ref.at[pl.ds(2 * rows, ID_ROWS)], ids_all.at[side, slot])
    for ref, span in zip(q_refs, spans):
        fetch(ref, q_all.at[span, pl.ds(0, width)])
    for side, side_refs in enumerate((own_refs, far_refs)):
        for ref, span in zip(side_refs, spans):
            fetch(ref.at[pl.ds(0, rows)], k_all.at[side, span, pl.ds(0, width)])
            fetch(ref.at[pl.ds(rows, rows)], v_all.at[side, span, pl.ds(0, width)])
    v_all[:, :, width:] = jnp.ones((2, pieces * rows, width), jnp.bfloat16)
    for copy in started[: 2 * pieces]:
        copy.wait()
    lane = lax.broadcasted_iota(jnp.int32, (width, width), 1)
    shift = jnp.minimum(lane // 2, 8)
    odd = lane % 2
    live = lane < 16
    for side in range(2):
        for piece in range(pieces):
            ids = ids_all[side, piece].astype(jnp.float32)
            for part in range(parts):
                line = jnp.broadcast_to(ids[part : part + 1], (width, width)).T.astype(jnp.int32)
                flag = lax.bitwise_xor(lax.bitwise_and(lax.shift_right_logical(line, shift), 1), odd)
                here = pl.ds(piece * rows + part * width, width)
                mark = jnp.where(live, flag.astype(jnp.float32), 0.0)
                k_all[side, here, width:] = mark.astype(jnp.bfloat16)
                if side == 0:
                    other = jnp.where(live, (flag.astype(jnp.float32) - 1.0) * MISMATCH, 0.0)
                    q_all[here, width:] = other.astype(jnp.bfloat16)
    for copy in started[2 * pieces :]:
        copy.wait()

    later = where_ref[1]
    far_bias = jnp.where(later > 0, 0.0, -MISMATCH * 4.0).astype(jnp.float32)
    factor = scale * math.log2(math.e)
    contract = (((1,), (1,)), ((), ()))
    for piece in range(pieces):
        span = (piece + 1) * rows
        for step in range(rows // tile):
            q = q_all[pl.ds(piece * rows + step * tile, tile), :]
            own = lax.dot_general(q, k_all[0, pl.ds(0, span), :], contract, preferred_element_type=jnp.float32)
            far = lax.dot_general(q, k_all[1, pl.ds(0, span), :], contract, preferred_element_type=jnp.float32)
            before = piece * rows
            row = lax.broadcasted_iota(jnp.int32, (tile, rows), 0) + step * tile
            column = lax.broadcasted_iota(jnp.int32, (tile, rows), 1)
            diagonal = jnp.where(column <= row, own[:, before:], -MISMATCH * 4.0)
            last = far[:, before:] + far_bias
            if piece:
                own = jnp.concatenate([own[:, :before], diagonal], axis=1)
                far = jnp.concatenate([far[:, :before], last], axis=1)
            else:
                own, far = diagonal, last
            top = jnp.maximum(own[:, :width], far[:, :width])
            for start in range(width, span, width):
                top = jnp.maximum(top, own[:, start : start + width])
                top = jnp.maximum(top, far[:, start : start + width])
            top = jnp.max(top, axis=1, keepdims=True) * factor
            own = jnp.exp2(own * factor - top).astype(jnp.bfloat16)
            far = jnp.exp2(far * factor - top).astype(jnp.bfloat16)
            total = jnp.dot(own, v_all[0, pl.ds(0, span), :], preferred_element_type=jnp.float32)
            total = total + jnp.dot(far, v_all[1, pl.ds(0, span), :], preferred_element_type=jnp.float32)
            result = total[:, :width] / total[:, width:]
            out_all[piece, pl.ds(step * tile, tile), :] = result.astype(jnp.bfloat16)
    started.clear()
    for ref, slot in zip(out_refs, slots):
        fetch(out_all.at[slot], ref)
    for copy in started:
        copy.wait()


def attend(where, kv_own, kv_far, q):
    pieces = len(q)
    rows, width = q[0].shape
    anywhere = pl.BlockSpec(memory_space=pl.ANY)
    return pl.pallas_call(
        lambda *refs: attend_kernel(1.0 / math.sqrt(width), *refs),
        out_shape=(jax.ShapeDtypeStruct((rows, width), jnp.bfloat16),) * pieces,
        in_specs=[pl.BlockSpec(memory_space=pltpu.SMEM)] + [anywhere] * (3 * pieces),
        out_specs=(anywhere,) * pieces,
        scratch_shapes=[
            pltpu.VMEM((2, pieces * rows, 2 * width), jnp.bfloat16),
            pltpu.VMEM((2, pieces * rows, 2 * width), jnp.bfloat16),
            pltpu.VMEM((pieces * rows, 2 * width), jnp.bfloat16),
            pltpu.VMEM((2, pieces, ID_ROWS, width), jnp.bfloat16),
            pltpu.VMEM((pieces, rows, width), jnp.bfloat16),
            pltpu.SemaphoreType.DMA((7 * pieces,)),
        ],
        compiler_params=pltpu.CompilerParams(vmem_limit_bytes=48 * 1024 * 1024),
        name="attend",
    )(where, *kv_own, *kv_far, *q)


def gather_rows(place, pieces, w_source, a_all, w_all, sems):
    rows, width = pieces[0].shape
    copies = [pltpu.make_async_copy(w_source, w_all, sems.at[len(pieces)])]
    for offset, ref in enumerate(pieces):
        head = lax.bitwise_xor(place, offset)
        columns = pl.ds(pl.multiple_of(head * width, width), width)
        copies.append(pltpu.make_async_copy(ref, a_all.at[:, columns], sems.at[offset]))
    for copy in copies:
        copy.start()
    for copy in copies:
        copy.wait()


def near_kernel(where_ref, w_ref, *refs):
    out_ref, a_all, w_all, sems = refs[-4:]
    half = w_all.shape[1]
    columns = pl.ds(pl.multiple_of(where_ref[2] // 2 * half, half), half)
    gather_rows(where_ref[0], refs[:-4], w_ref.at[:, columns], a_all, w_all, sems)
    out_ref[...] = jnp.dot(a_all[...], w_all[...], preferred_element_type=jnp.float32)


def far_kernel(where_ref, w_ref, near_ref, *refs):
    mine_ref, other_ref, a_all, w_all, total, sems = refs[-6:]
    gather_rows(where_ref[0], refs[:-6], w_ref, a_all, w_all, sems)
    total[...] = near_ref[...] + jnp.dot(a_all[...], w_all[...], preferred_element_type=jnp.float32)
    width = mine_ref.shape[1]
    core = where_ref[2] % 2
    mine_ref[...] = total[:, pl.ds(pl.multiple_of(core * width, width), width)]
    other_ref[...] = total[:, pl.ds(pl.multiple_of((1 - core) * width, width), width)].astype(jnp.bfloat16)


def near_sums(where, out_weight, pieces):
    rows, width = pieces[0].shape
    depth, half = out_weight.shape[0], out_weight.shape[1] // 2
    anywhere = pl.BlockSpec(memory_space=pl.ANY)
    return pl.pallas_call(
        near_kernel,
        out_shape=jax.ShapeDtypeStruct((rows, half), jnp.float32),
        in_specs=[pl.BlockSpec(memory_space=pltpu.SMEM)] + [anywhere] * (1 + len(pieces)),
        out_specs=pl.BlockSpec(memory_space=pltpu.VMEM),
        scratch_shapes=[
            pltpu.VMEM((rows, depth), jnp.bfloat16),
            pltpu.VMEM((depth, half), jnp.bfloat16),
            pltpu.SemaphoreType.DMA((1 + len(pieces),)),
        ],
        compiler_params=pltpu.CompilerParams(vmem_limit_bytes=24 * 1024 * 1024),
        name="near_sums",
    )(where, out_weight, *pieces)


def far_sums(where, weights, near, pieces):
    rows, width = pieces[0].shape
    depth, half = weights.shape
    anywhere = pl.BlockSpec(memory_space=pl.ANY)
    local_memory = pl.BlockSpec(memory_space=pltpu.VMEM)
    return pl.pallas_call(
        far_kernel,
        out_shape=(
            jax.ShapeDtypeStruct((rows, half // 2), jnp.float32),
            jax.ShapeDtypeStruct((rows, half // 2), jnp.bfloat16),
        ),
        in_specs=[pl.BlockSpec(memory_space=pltpu.SMEM), anywhere, local_memory] + [anywhere] * len(pieces),
        out_specs=(local_memory, local_memory),
        scratch_shapes=[
            pltpu.VMEM((rows, depth), jnp.bfloat16),
            pltpu.VMEM((depth, half), jnp.bfloat16),
            pltpu.VMEM((rows, half), jnp.float32),
            pltpu.SemaphoreType.DMA((1 + len(pieces),)),
        ],
        compiler_params=pltpu.CompilerParams(vmem_limit_bytes=24 * 1024 * 1024),
        name="far_sums",
    )(where, weights, near, *pieces)


def head_plan(queries, keys, values, cluster_ids, out_weight):
    heads = cluster_ids.shape[0]
    seq = lax.axis_index("seq").astype(jnp.int32)
    here = lax.axis_index("head").astype(jnp.int32)
    where = jnp.stack([seq // 2, seq % 2, here])

    def swap(array, axis, bits):
        size = lax.axis_size(axis)
        return lax.ppermute(array, axis, [(place, place ^ bits) for place in range(size)])

    def after(array, *others):
        return lax.optimization_barrier((array,) + others)[0]

    q, kv = pack(where, queries, keys, values, cluster_ids)
    kv_own, kv_far, q_own = [kv[0]] + [None] * 3, [None] * 4, [q[0]] + [None] * 3
    kv_own[2] = swap(kv[2], "seq", 4)
    kv_own[1] = swap(kv[1], "seq", 2)
    kv_far[0] = swap(kv[0], "seq", 1)
    kv_own[3] = swap(after(kv[3], kv_own[1]), "seq", 6)
    half = out_weight.shape[1] // 2
    weights = lax.dynamic_slice_in_dim(after(out_weight, kv[1]), (1 - here // 2) * half, half, 1)
    weights = swap(weights, "head", 2)
    for offset in (1, 2, 3):
        kv_far[offset] = swap(kv_own[offset], "seq", 1)
    q_own[2] = swap(after(q[2], kv_own[2]), "seq", 4)
    for offset in (3, 1):
        q_own[offset] = swap(after(q[offset], kv_own[3]), "seq", 2 * offset)
    attended = list(attend(where, kv_own, kv_far, q_own))
    for offset in range(1, heads):
        attended[offset] = swap(attended[offset], "seq", 2 * offset)
    across = [swap(piece, "head", 2) for piece in attended]
    near = near_sums(where, out_weight, attended)
    mine, other = far_sums(where, weights, near, across)
    return (mine + swap(other, "head", 1).astype(jnp.float32)).astype(jnp.bfloat16)


def local(queries, keys, values, cluster_ids, out_weight):
    groups = cluster_ids.shape[0]
    if lax.axis_size("seq") == 2 * groups and lax.axis_size("head") == 4:
        return head_plan(queries, keys, values, cluster_ids, out_weight)
    return padded_plan(queries, keys, values, cluster_ids, out_weight)


def solution(mesh):
    placed = (
        P("seq", "head"),
        P("seq", "head"),
        P("seq", "head"),
        P("head", "seq"),
        P("head", None),
    )
    return jax.shard_map(
        local, mesh=mesh, in_specs=placed, out_specs=P("seq", "head"), check_vma=False
    )
```

```python
import math

import jax
import jax.numpy as jnp
from jax import lax
from jax.experimental import pallas as pl
from jax.experimental.pallas import tpu as pltpu
from jax.sharding import PartitionSpec as P

CLUSTERS = 256
MOST = 4


def attend_block(query_part, key_part, value_part, filled_part, score_scale):
    owners, local_slots, head_width = query_part.shape
    local_count = filled_part.shape[1]
    slot_count = local_slots // local_count
    query_rows = query_part.reshape(owners, local_count, slot_count, head_width)
    key_rows = key_part.reshape(owners, local_count, slot_count, head_width)
    value_rows = value_part.reshape(owners, local_count, slot_count, head_width)
    scores = (
        jnp.einsum("scmd,tcnd->csmtn", query_rows, key_rows, preferred_element_type=jnp.float32)
        * score_scale
    )
    order_index = jnp.arange(owners * slot_count, dtype=jnp.int32).reshape(owners, slot_count)
    before = order_index[None, None, :, :] <= order_index[:, :, None, None]
    itself = order_index[None, None, :, :] == order_index[:, :, None, None]
    slot_value = jnp.arange(slot_count, dtype=jnp.float32)[None, None, :]
    taken_slot = slot_value < jnp.transpose(filled_part).astype(jnp.float32)[:, :, None]
    allowed = before[None] & (taken_slot[:, None, None, :, :] | itself[None])
    scores = jnp.where(allowed, scores, -1e30)
    row_top = jnp.max(scores, axis=(3, 4), keepdims=True)
    spread = jnp.exp(scores - row_top)
    weights = (spread / jnp.sum(spread, axis=(3, 4), keepdims=True)).astype(jnp.bfloat16)
    combined = jnp.einsum(
        "csmtn,tcnd->scmd", weights, value_rows, preferred_element_type=jnp.float32
    )
    return combined.astype(jnp.bfloat16).reshape(owners, local_slots, head_width)


def padded_plan(queries, keys, values, cluster_ids, out_weight):
    token_count = queries.shape[0]
    groups = cluster_ids.shape[0]
    head_width = queries.shape[1] // groups
    owners = lax.axis_size("seq")
    local_count = CLUSTERS // owners
    position = jnp.arange(token_count, dtype=jnp.int32)
    earlier = position[None, :] < position[:, None]
    matching = cluster_ids[:, :, None] == cluster_ids[:, None, :]
    slot_rank = jnp.sum((matching & earlier[None]).astype(jnp.int32), axis=2)
    owner_index = jnp.transpose(cluster_ids // local_count)
    within_owner = jnp.transpose(cluster_ids % local_count * MOST + slot_rank)
    head_index = jnp.arange(groups, dtype=jnp.int32)[None, :]

    def place(source):
        shaped = source.reshape(token_count, groups, head_width)
        blank = jnp.zeros((owners, groups, local_count * MOST, head_width), jnp.bfloat16)
        return blank.at[owner_index, head_index, within_owner].set(shaped)

    cluster_axis = jnp.arange(CLUSTERS, dtype=jnp.int32)
    filled = jnp.sum(
        (cluster_ids[:, :, None] == cluster_axis[None, None, :]).astype(jnp.int32), axis=1
    )
    filled = jnp.transpose(filled.reshape(groups, owners, local_count), (1, 0, 2)).astype(
        jnp.bfloat16
    )
    score_scale = 1.0 / math.sqrt(head_width)
    query_in = lax.all_to_all(place(queries), "seq", split_axis=0, concat_axis=0, tiled=True)
    key_in = lax.all_to_all(place(keys), "seq", split_axis=0, concat_axis=0, tiled=True)
    value_in = lax.all_to_all(place(values), "seq", split_axis=0, concat_axis=0, tiled=True)
    count_in = lax.all_to_all(filled, "seq", split_axis=0, concat_axis=0, tiled=True)

    def one_head(position_head):
        return attend_block(
            lax.dynamic_index_in_dim(query_in, position_head, 1, False),
            lax.dynamic_index_in_dim(key_in, position_head, 1, False),
            lax.dynamic_index_in_dim(value_in, position_head, 1, False),
            lax.dynamic_index_in_dim(count_in, position_head, 1, False),
            score_scale,
        )

    results = lax.map(one_head, jnp.arange(query_in.shape[1], dtype=jnp.int32))
    returned = lax.all_to_all(results, "seq", split_axis=1, concat_axis=1, tiled=True)
    gathered = returned[head_index, owner_index, within_owner]
    attended = gathered.reshape(token_count, groups * head_width)
    partial_sums = jnp.dot(attended, out_weight, preferred_element_type=jnp.float32)
    summed = lax.psum_scatter(partial_sums, "head", scatter_dimension=1, tiled=True)
    return summed.astype(jnp.bfloat16)


ID_ROWS = 16
MISMATCH = 262144.0


def coordinates():
    seq = lax.axis_index("seq").astype(jnp.int32)
    return seq // 2, seq % 2, lax.axis_index("head").astype(jnp.int32)


def pack_kernel(q_ref, k_ref, v_ref, ids_ref, *outs):
    heads = ids_ref.shape[0]
    rows, width = outs[0].shape
    parts = rows // width
    place = coordinates()[0]
    for offset in range(heads):
        q_out, kv_out = outs[2 * offset], outs[2 * offset + 1]
        head = lax.bitwise_xor(place, offset)
        columns = pl.ds(pl.multiple_of(head * width, width), width)
        kv_out[pl.ds(0, rows), :] = k_ref[:, columns]
        kv_out[pl.ds(rows, rows), :] = v_ref[:, columns]
        q_out[...] = q_ref[:, columns]
        ids = ids_ref[pl.ds(head, 1), :].astype(jnp.float32)
        lines = [ids[:, part * width : (part + 1) * width] for part in range(parts)]
        lines.append(jnp.zeros((ID_ROWS - parts, width), jnp.float32))
        kv_out[pl.ds(2 * rows, ID_ROWS), :] = jnp.concatenate(lines, axis=0).astype(jnp.bfloat16)


def pack(queries, keys, values, cluster_ids):
    heads = cluster_ids.shape[0]
    rows = queries.shape[0]
    width = queries.shape[1] // heads
    local_memory = pl.BlockSpec(memory_space=pltpu.VMEM)
    pair = [
        jax.ShapeDtypeStruct((rows, width), jnp.bfloat16),
        jax.ShapeDtypeStruct((2 * rows + ID_ROWS, width), jnp.bfloat16),
    ]
    outs = pl.pallas_call(
        pack_kernel,
        out_shape=tuple(pair * heads),
        in_specs=[local_memory] * 4,
        out_specs=(local_memory,) * (2 * heads),
        cost_estimate=pl.CostEstimate(flops=2700000000, bytes_accessed=8910000, transcendentals=0),
        name="pack",
    )(queries, keys, values, cluster_ids)
    return outs[0::2], outs[1::2]


def attend_kernel(scale, *refs):
    place, later, _ = coordinates()
    pieces = (len(refs) - 6) // 4
    own_refs, far_refs, q_refs, out_refs = (refs[pieces * kind : pieces * (kind + 1)] for kind in range(4))
    k_all, v_all, q_all, ids_all, out_all, sems = refs[4 * pieces :]
    rows, width = q_refs[0].shape
    parts = rows // width
    tile = 256
    started = []
    slots = [lax.bitwise_xor(place, offset) for offset in range(pieces)]
    spans = [pl.ds(pl.multiple_of(slot * rows, rows), rows) for slot in slots]

    def fetch(source, target):
        copy = pltpu.make_async_copy(source, target, sems.at[len(started)])
        copy.start()
        started.append(copy)

    for side, side_refs in enumerate((own_refs, far_refs)):
        for ref, slot in zip(side_refs, slots):
            fetch(ref.at[pl.ds(2 * rows, ID_ROWS)], ids_all.at[side, slot])
    for ref, span in zip(q_refs, spans):
        fetch(ref, q_all.at[span, pl.ds(0, width)])
    for side, side_refs in enumerate((own_refs, far_refs)):
        for ref, span in zip(side_refs, spans):
            fetch(ref.at[pl.ds(0, rows)], k_all.at[side, span, pl.ds(0, width)])
            fetch(ref.at[pl.ds(rows, rows)], v_all.at[side, span, pl.ds(0, width)])
    v_all[:, :, width:] = jnp.ones((2, pieces * rows, width), jnp.bfloat16)
    for copy in started[: 2 * pieces]:
        copy.wait()
    lane = lax.broadcasted_iota(jnp.int32, (width, width), 1)
    shift = jnp.minimum(lane // 2, 8)
    odd = lane % 2
    live = lane < 16
    for side in range(2):
        for piece in range(pieces):
            ids = ids_all[side, piece].astype(jnp.float32)
            for part in range(parts):
                line = jnp.broadcast_to(ids[part : part + 1], (width, width)).T.astype(jnp.int32)
                flag = lax.bitwise_xor(lax.bitwise_and(lax.shift_right_logical(line, shift), 1), odd)
                here = pl.ds(piece * rows + part * width, width)
                mark = jnp.where(live, flag.astype(jnp.float32), 0.0)
                k_all[side, here, width:] = mark.astype(jnp.bfloat16)
                if side == 0:
                    other = jnp.where(live, (flag.astype(jnp.float32) - 1.0) * MISMATCH, 0.0)
                    q_all[here, width:] = other.astype(jnp.bfloat16)
    for copy in started[2 * pieces :]:
        copy.wait()

    far_bias = jnp.where(later > 0, 0.0, -MISMATCH * 4.0).astype(jnp.float32)
    factor = scale * math.log2(math.e)
    contract = (((1,), (1,)), ((), ()))
    for piece in range(pieces):
        span = (piece + 1) * rows
        for step in range(rows // tile):
            q = q_all[pl.ds(piece * rows + step * tile, tile), :]
            own = lax.dot_general(q, k_all[0, pl.ds(0, span), :], contract, preferred_element_type=jnp.float32)
            far = lax.dot_general(q, k_all[1, pl.ds(0, span), :], contract, preferred_element_type=jnp.float32)
            before = piece * rows
            row = lax.broadcasted_iota(jnp.int32, (tile, rows), 0) + step * tile
            column = lax.broadcasted_iota(jnp.int32, (tile, rows), 1)
            diagonal = jnp.where(column <= row, own[:, before:], -MISMATCH * 4.0)
            last = far[:, before:] + far_bias
            if piece:
                own = jnp.concatenate([own[:, :before], diagonal], axis=1)
                far = jnp.concatenate([far[:, :before], last], axis=1)
            else:
                own, far = diagonal, last
            top = jnp.maximum(own[:, :width], far[:, :width])
            for start in range(width, span, width):
                top = jnp.maximum(top, own[:, start : start + width])
                top = jnp.maximum(top, far[:, start : start + width])
            top = jnp.max(top, axis=1, keepdims=True) * factor
            own = jnp.exp2(own * factor - top).astype(jnp.bfloat16)
            far = jnp.exp2(far * factor - top).astype(jnp.bfloat16)
            total = jnp.dot(own, v_all[0, pl.ds(0, span), :], preferred_element_type=jnp.float32)
            total = total + jnp.dot(far, v_all[1, pl.ds(0, span), :], preferred_element_type=jnp.float32)
            result = total[:, :width] / total[:, width:]
            out_all[piece, pl.ds(step * tile, tile), :] = result.astype(jnp.bfloat16)
    started.clear()
    for ref, slot in zip(out_refs, slots):
        fetch(out_all.at[slot], ref)
    for copy in started:
        copy.wait()


def attend(kv_own, kv_far, q):
    pieces = len(q)
    rows, width = q[0].shape
    anywhere = pl.BlockSpec(memory_space=pl.ANY)
    return pl.pallas_call(
        lambda *refs: attend_kernel(1.0 / math.sqrt(width), *refs),
        out_shape=(jax.ShapeDtypeStruct((rows, width), jnp.bfloat16),) * pieces,
        in_specs=[anywhere] * (3 * pieces),
        out_specs=(anywhere,) * pieces,
        scratch_shapes=[
            pltpu.VMEM((2, pieces * rows, 2 * width), jnp.bfloat16),
            pltpu.VMEM((2, pieces * rows, 2 * width), jnp.bfloat16),
            pltpu.VMEM((pieces * rows, 2 * width), jnp.bfloat16),
            pltpu.VMEM((2, pieces, ID_ROWS, width), jnp.bfloat16),
            pltpu.VMEM((pieces, rows, width), jnp.bfloat16),
            pltpu.SemaphoreType.DMA((7 * pieces,)),
        ],
        compiler_params=pltpu.CompilerParams(vmem_limit_bytes=48 * 1024 * 1024),
        cost_estimate=pl.CostEstimate(flops=11600000000, bytes_accessed=38280000, transcendentals=0),
        name="attend",
    )(*kv_own, *kv_far, *q)


def gather_rows(place, pieces, w_source, a_all, w_all, sems):
    rows, width = pieces[0].shape
    copies = [pltpu.make_async_copy(w_source, w_all, sems.at[len(pieces)])]
    for offset, ref in enumerate(pieces):
        head = lax.bitwise_xor(place, offset)
        columns = pl.ds(pl.multiple_of(head * width, width), width)
        copies.append(pltpu.make_async_copy(ref, a_all.at[:, columns], sems.at[offset]))
    for copy in copies:
        copy.start()
    for copy in copies:
        copy.wait()


def near_kernel(w_ref, *refs):
    out_ref, a_all, w_all, sems = refs[-4:]
    half = w_all.shape[1]
    place, _, here = coordinates()
    columns = pl.ds(pl.multiple_of(here // 2 * half, half), half)
    gather_rows(place, refs[:-4], w_ref.at[:, columns], a_all, w_all, sems)
    out_ref[...] = jnp.dot(a_all[...], w_all[...], preferred_element_type=jnp.float32)


def far_kernel(w_ref, near_ref, *refs):
    place, _, here = coordinates()
    mine_ref, other_ref, a_all, w_all, total, sems = refs[-6:]
    gather_rows(place, refs[:-6], w_ref, a_all, w_all, sems)
    total[...] = near_ref[...] + jnp.dot(a_all[...], w_all[...], preferred_element_type=jnp.float32)
    width = mine_ref.shape[1]
    core = here % 2
    mine_ref[...] = total[:, pl.ds(pl.multiple_of(core * width, width), width)]
    other_ref[...] = total[:, pl.ds(pl.multiple_of((1 - core) * width, width), width)].astype(jnp.bfloat16)


def near_sums(out_weight, pieces):
    rows, width = pieces[0].shape
    depth, half = out_weight.shape[0], out_weight.shape[1] // 2
    anywhere = pl.BlockSpec(memory_space=pl.ANY)
    return pl.pallas_call(
        near_kernel,
        out_shape=jax.ShapeDtypeStruct((rows, half), jnp.float32),
        in_specs=[anywhere] * (1 + len(pieces)),
        out_specs=pl.BlockSpec(memory_space=pltpu.VMEM),
        scratch_shapes=[
            pltpu.VMEM((rows, depth), jnp.bfloat16),
            pltpu.VMEM((depth, half), jnp.bfloat16),
            pltpu.SemaphoreType.DMA((1 + len(pieces),)),
        ],
        compiler_params=pltpu.CompilerParams(vmem_limit_bytes=24 * 1024 * 1024),
        cost_estimate=pl.CostEstimate(flops=1500000000, bytes_accessed=4950000, transcendentals=0),
        name="near_sums",
    )(out_weight, *pieces)


def far_sums(weights, near, pieces):
    rows, width = pieces[0].shape
    depth, half = weights.shape
    anywhere = pl.BlockSpec(memory_space=pl.ANY)
    local_memory = pl.BlockSpec(memory_space=pltpu.VMEM)
    return pl.pallas_call(
        far_kernel,
        out_shape=(
            jax.ShapeDtypeStruct((rows, half // 2), jnp.float32),
            jax.ShapeDtypeStruct((rows, half // 2), jnp.bfloat16),
        ),
        in_specs=[anywhere, local_memory] + [anywhere] * len(pieces),
        out_specs=(local_memory, local_memory),
        scratch_shapes=[
            pltpu.VMEM((rows, depth), jnp.bfloat16),
            pltpu.VMEM((depth, half), jnp.bfloat16),
            pltpu.VMEM((rows, half), jnp.float32),
            pltpu.SemaphoreType.DMA((1 + len(pieces),)),
        ],
        compiler_params=pltpu.CompilerParams(vmem_limit_bytes=24 * 1024 * 1024),
        cost_estimate=pl.CostEstimate(flops=1800000000, bytes_accessed=5940000, transcendentals=0),
        name="far_sums",
    )(weights, near, *pieces)


def head_plan(queries, keys, values, cluster_ids, out_weight):
    heads = cluster_ids.shape[0]
    here = lax.axis_index("head").astype(jnp.int32)

    def swap(array, axis, bits):
        size = lax.axis_size(axis)
        return lax.ppermute(array, axis, [(place, place ^ bits) for place in range(size)])

    def after(array, *others):
        return lax.optimization_barrier((array,) + others)[0]

    q, kv = pack(queries, keys, values, cluster_ids)
    kv_own, kv_far, q_own = [kv[0]] + [None] * 3, [None] * 4, [q[0]] + [None] * 3
    kv_own[2] = swap(kv[2], "seq", 4)
    kv_own[1] = swap(kv[1], "seq", 2)
    kv_far[0] = swap(kv[0], "seq", 1)
    kv_own[3] = swap(after(kv[3], kv_own[1]), "seq", 6)
    half = out_weight.shape[1] // 2
    weights = lax.dynamic_slice_in_dim(after(out_weight, kv[1]), (1 - here // 2) * half, half, 1)
    weights = swap(weights, "head", 2)
    for offset in (1, 2, 3):
        kv_far[offset] = swap(kv_own[offset], "seq", 1)
    q_own[2] = swap(after(q[2], kv_own[2]), "seq", 4)
    for offset in (3, 1):
        q_own[offset] = swap(after(q[offset], kv_own[3]), "seq", 2 * offset)
    attended = list(attend(kv_own, kv_far, q_own))
    for offset in range(1, heads):
        attended[offset] = swap(attended[offset], "seq", 2 * offset)
    across = [swap(piece, "head", 2) for piece in attended]
    near = near_sums(out_weight, attended)
    mine, other = far_sums(weights, near, across)
    return (mine + swap(other, "head", 1).astype(jnp.float32)).astype(jnp.bfloat16)


def local(queries, keys, values, cluster_ids, out_weight):
    groups = cluster_ids.shape[0]
    if lax.axis_size("seq") == 2 * groups and lax.axis_size("head") == 4:
        return head_plan(queries, keys, values, cluster_ids, out_weight)
    return padded_plan(queries, keys, values, cluster_ids, out_weight)


def solution(mesh):
    placed = (
        P("seq", "head"),
        P("seq", "head"),
        P("seq", "head"),
        P("head", "seq"),
        P("head", None),
    )
    return jax.shard_map(
        local, mesh=mesh, in_specs=placed, out_specs=P("seq", "head"), check_vma=False
    )
```

```python
import math

import jax
import jax.numpy as jnp
from jax import lax
from jax.experimental import pallas as pl
from jax.experimental.pallas import tpu as pltpu
from jax.sharding import PartitionSpec as P

CLUSTERS = 256
MOST = 4


def attend_block(query_part, key_part, value_part, filled_part, score_scale):
    owners, local_slots, head_width = query_part.shape
    local_count = filled_part.shape[1]
    slot_count = local_slots // local_count
    query_rows = query_part.reshape(owners, local_count, slot_count, head_width)
    key_rows = key_part.reshape(owners, local_count, slot_count, head_width)
    value_rows = value_part.reshape(owners, local_count, slot_count, head_width)
    scores = (
        jnp.einsum("scmd,tcnd->csmtn", query_rows, key_rows, preferred_element_type=jnp.float32)
        * score_scale
    )
    order_index = jnp.arange(owners * slot_count, dtype=jnp.int32).reshape(owners, slot_count)
    before = order_index[None, None, :, :] <= order_index[:, :, None, None]
    itself = order_index[None, None, :, :] == order_index[:, :, None, None]
    slot_value = jnp.arange(slot_count, dtype=jnp.float32)[None, None, :]
    taken_slot = slot_value < jnp.transpose(filled_part).astype(jnp.float32)[:, :, None]
    allowed = before[None] & (taken_slot[:, None, None, :, :] | itself[None])
    scores = jnp.where(allowed, scores, -1e30)
    row_top = jnp.max(scores, axis=(3, 4), keepdims=True)
    spread = jnp.exp(scores - row_top)
    weights = (spread / jnp.sum(spread, axis=(3, 4), keepdims=True)).astype(jnp.bfloat16)
    combined = jnp.einsum(
        "csmtn,tcnd->scmd", weights, value_rows, preferred_element_type=jnp.float32
    )
    return combined.astype(jnp.bfloat16).reshape(owners, local_slots, head_width)


def padded_plan(queries, keys, values, cluster_ids, out_weight):
    token_count = queries.shape[0]
    groups = cluster_ids.shape[0]
    head_width = queries.shape[1] // groups
    owners = lax.axis_size("seq")
    local_count = CLUSTERS // owners
    position = jnp.arange(token_count, dtype=jnp.int32)
    earlier = position[None, :] < position[:, None]
    matching = cluster_ids[:, :, None] == cluster_ids[:, None, :]
    slot_rank = jnp.sum((matching & earlier[None]).astype(jnp.int32), axis=2)
    owner_index = jnp.transpose(cluster_ids // local_count)
    within_owner = jnp.transpose(cluster_ids % local_count * MOST + slot_rank)
    head_index = jnp.arange(groups, dtype=jnp.int32)[None, :]

    def place(source):
        shaped = source.reshape(token_count, groups, head_width)
        blank = jnp.zeros((owners, groups, local_count * MOST, head_width), jnp.bfloat16)
        return blank.at[owner_index, head_index, within_owner].set(shaped)

    cluster_axis = jnp.arange(CLUSTERS, dtype=jnp.int32)
    filled = jnp.sum(
        (cluster_ids[:, :, None] == cluster_axis[None, None, :]).astype(jnp.int32), axis=1
    )
    filled = jnp.transpose(filled.reshape(groups, owners, local_count), (1, 0, 2)).astype(
        jnp.bfloat16
    )
    score_scale = 1.0 / math.sqrt(head_width)
    query_in = lax.all_to_all(place(queries), "seq", split_axis=0, concat_axis=0, tiled=True)
    key_in = lax.all_to_all(place(keys), "seq", split_axis=0, concat_axis=0, tiled=True)
    value_in = lax.all_to_all(place(values), "seq", split_axis=0, concat_axis=0, tiled=True)
    count_in = lax.all_to_all(filled, "seq", split_axis=0, concat_axis=0, tiled=True)

    def one_head(position_head):
        return attend_block(
            lax.dynamic_index_in_dim(query_in, position_head, 1, False),
            lax.dynamic_index_in_dim(key_in, position_head, 1, False),
            lax.dynamic_index_in_dim(value_in, position_head, 1, False),
            lax.dynamic_index_in_dim(count_in, position_head, 1, False),
            score_scale,
        )

    results = lax.map(one_head, jnp.arange(query_in.shape[1], dtype=jnp.int32))
    returned = lax.all_to_all(results, "seq", split_axis=1, concat_axis=1, tiled=True)
    gathered = returned[head_index, owner_index, within_owner]
    attended = gathered.reshape(token_count, groups * head_width)
    partial_sums = jnp.dot(attended, out_weight, preferred_element_type=jnp.float32)
    summed = lax.psum_scatter(partial_sums, "head", scatter_dimension=1, tiled=True)
    return summed.astype(jnp.bfloat16)


ID_ROWS = 16
MISMATCH = 262144.0


def coordinates():
    seq = lax.axis_index("seq").astype(jnp.int32)
    return seq // 2, seq % 2, lax.axis_index("head").astype(jnp.int32)


def pack_kernel(q_ref, k_ref, v_ref, ids_ref, *outs):
    heads = ids_ref.shape[0]
    rows, width = outs[0].shape
    parts = rows // width
    place = coordinates()[0]
    for offset in range(heads):
        q_out, kv_out = outs[2 * offset], outs[2 * offset + 1]
        head = lax.bitwise_xor(place, offset)
        columns = pl.ds(pl.multiple_of(head * width, width), width)
        kv_out[pl.ds(0, rows), :] = k_ref[:, columns]
        kv_out[pl.ds(rows, rows), :] = v_ref[:, columns]
        q_out[...] = q_ref[:, columns]
        ids = ids_ref[pl.ds(head, 1), :].astype(jnp.float32)
        lines = [ids[:, part * width : (part + 1) * width] for part in range(parts)]
        lines.append(jnp.zeros((ID_ROWS - parts, width), jnp.float32))
        kv_out[pl.ds(2 * rows, ID_ROWS), :] = jnp.concatenate(lines, axis=0).astype(jnp.bfloat16)


def pack(queries, keys, values, cluster_ids):
    heads = cluster_ids.shape[0]
    rows = queries.shape[0]
    width = queries.shape[1] // heads
    local_memory = pl.BlockSpec(memory_space=pltpu.VMEM)
    pair = [
        jax.ShapeDtypeStruct((rows, width), jnp.bfloat16),
        jax.ShapeDtypeStruct((2 * rows + ID_ROWS, width), jnp.bfloat16),
    ]
    outs = pl.pallas_call(
        pack_kernel,
        out_shape=tuple(pair * heads),
        in_specs=[local_memory] * 4,
        out_specs=(local_memory,) * (2 * heads),
        cost_estimate=pl.CostEstimate(flops=2700000000, bytes_accessed=8910000, transcendentals=0),
        name="pack",
    )(queries, keys, values, cluster_ids)
    return outs[0::2], outs[1::2]


def attend_kernel(scale, *refs):
    place, later, _ = coordinates()
    pieces = (len(refs) - 6) // 4
    own_refs, far_refs, q_refs, out_refs = (refs[pieces * kind : pieces * (kind + 1)] for kind in range(4))
    k_all, v_all, q_all, ids_all, out_all, sems = refs[4 * pieces :]
    rows, width = q_refs[0].shape
    parts = rows // width
    tile = 256
    slots = [lax.bitwise_xor(place, offset) for offset in range(pieces)]
    sides = (own_refs, far_refs)

    def copies_of(offset, slot):
        span = pl.ds(slot * rows if isinstance(slot, int) else pl.multiple_of(slot * rows, rows), rows)
        pairs = []
        for side, side_refs in enumerate(sides):
            ref = side_refs[offset]
            pairs.append((ref.at[pl.ds(2 * rows, ID_ROWS)], ids_all.at[side, slot]))
        pairs.append((q_refs[offset], q_all.at[span, pl.ds(0, width)]))
        for side, side_refs in enumerate(sides):
            ref = side_refs[offset]
            pairs.append((ref.at[pl.ds(0, rows)], k_all.at[side, span, pl.ds(0, width)]))
            pairs.append((ref.at[pl.ds(rows, rows)], v_all.at[side, span, pl.ds(0, width)]))
        return [
            pltpu.make_async_copy(source, target, sems.at[kind, slot]) for kind, (source, target) in enumerate(pairs)
        ]

    for offset, slot in enumerate(slots):
        for copy in copies_of(offset, slot):
            copy.start()
    v_all[:, :, width:] = jnp.ones((2, pieces * rows, width), jnp.bfloat16)
    lane = lax.broadcasted_iota(jnp.int32, (width, width), 1)
    shift = jnp.minimum(lane // 2, 8)
    odd = lane % 2
    live = lane < 16
    far_bias = jnp.where(later > 0, 0.0, -MISMATCH * 4.0).astype(jnp.float32)
    factor = scale * math.log2(math.e)
    contract = (((1,), (1,)), ((), ()))
    row = lax.broadcasted_iota(jnp.int32, (tile, tile), 0)
    column = lax.broadcasted_iota(jnp.int32, (tile, tile), 1)

    def ready(piece):
        waits = copies_of(0, piece)
        for copy in waits[:2]:
            copy.wait()
        for side in range(2):
            ids = ids_all[side, piece].astype(jnp.float32)
            for part in range(parts):
                line = jnp.broadcast_to(ids[part : part + 1], (width, width)).T.astype(jnp.int32)
                flag = lax.bitwise_xor(lax.bitwise_and(lax.shift_right_logical(line, shift), 1), odd)
                here = pl.ds(piece * rows + part * width, width)
                mark = jnp.where(live, flag.astype(jnp.float32), 0.0)
                k_all[side, here, width:] = mark.astype(jnp.bfloat16)
                if side == 0:
                    other = jnp.where(live, (flag.astype(jnp.float32) - 1.0) * MISMATCH, 0.0)
                    q_all[here, width:] = other.astype(jnp.bfloat16)
        for copy in waits[2:]:
            copy.wait()

    def scores_of(piece, step):
        edge = piece * rows + step * tile
        q = q_all[pl.ds(edge, tile), :]
        own = lax.dot_general(q, k_all[0, pl.ds(0, edge + tile), :], contract, preferred_element_type=jnp.float32)
        far = lax.dot_general(
            q, k_all[1, pl.ds(0, (piece + 1) * rows), :], contract, preferred_element_type=jnp.float32
        )
        return own, far

    def finish(piece, step, own, far):
        before = piece * rows
        edge = before + step * tile
        diagonal = jnp.where(column <= row, own[:, edge:], -MISMATCH * 4.0)
        last = far[:, before:] + far_bias
        own = jnp.concatenate([own[:, :edge], diagonal], axis=1) if edge else diagonal
        far = jnp.concatenate([far[:, :before], last], axis=1) if before else last
        top = own[:, :width]
        for start in range(width, own.shape[1], width):
            top = jnp.maximum(top, own[:, start : start + width])
        for start in range(0, far.shape[1], width):
            top = jnp.maximum(top, far[:, start : start + width])
        top = jnp.max(top, axis=1, keepdims=True) * factor
        own = jnp.exp2(own * factor - top).astype(jnp.bfloat16)
        far = jnp.exp2(far * factor - top).astype(jnp.bfloat16)
        total = jnp.dot(own, v_all[0, pl.ds(0, own.shape[1]), :], preferred_element_type=jnp.float32)
        total = total + jnp.dot(far, v_all[1, pl.ds(0, far.shape[1]), :], preferred_element_type=jnp.float32)
        result = total[:, :width] / total[:, width:]
        out_all[piece, pl.ds(step * tile, tile), :] = result.astype(jnp.bfloat16)

    pending = None
    for piece in range(pieces):
        ready(piece)
    for piece in range(pieces):
        for step in range(rows // tile):
            scores = scores_of(piece, step)
            if pending is not None:
                finish(*pending)
            pending = (piece, step) + scores
    finish(*pending)
    copies = [
        pltpu.make_async_copy(out_all.at[slot], ref, sems.at[0, offset])
        for offset, (slot, ref) in enumerate(zip(slots, out_refs))
    ]
    for copy in copies:
        copy.start()
    for copy in copies:
        copy.wait()


def attend(kv_own, kv_far, q):
    pieces = len(q)
    rows, width = q[0].shape
    anywhere = pl.BlockSpec(memory_space=pl.ANY)
    return pl.pallas_call(
        lambda *refs: attend_kernel(1.0 / math.sqrt(width), *refs),
        out_shape=(jax.ShapeDtypeStruct((rows, width), jnp.bfloat16),) * pieces,
        in_specs=[anywhere] * (3 * pieces),
        out_specs=(anywhere,) * pieces,
        scratch_shapes=[
            pltpu.VMEM((2, pieces * rows, 2 * width), jnp.bfloat16),
            pltpu.VMEM((2, pieces * rows, 2 * width), jnp.bfloat16),
            pltpu.VMEM((pieces * rows, 2 * width), jnp.bfloat16),
            pltpu.VMEM((2, pieces, ID_ROWS, width), jnp.bfloat16),
            pltpu.VMEM((pieces, rows, width), jnp.bfloat16),
            pltpu.SemaphoreType.DMA((7, pieces)),
        ],
        compiler_params=pltpu.CompilerParams(vmem_limit_bytes=48 * 1024 * 1024),
        cost_estimate=pl.CostEstimate(flops=4000000000, bytes_accessed=13200000, transcendentals=0),
        name="attend",
    )(*kv_own, *kv_far, *q)


def gather_rows(place, pieces, w_source, a_all, w_all, sems):
    rows, width = pieces[0].shape
    copies = [pltpu.make_async_copy(w_source, w_all, sems.at[len(pieces)])]
    for offset, ref in enumerate(pieces):
        head = lax.bitwise_xor(place, offset)
        columns = pl.ds(pl.multiple_of(head * width, width), width)
        copies.append(pltpu.make_async_copy(ref, a_all.at[:, columns], sems.at[offset]))
    for copy in copies:
        copy.start()
    for copy in copies:
        copy.wait()


def near_kernel(w_ref, *refs):
    out_ref, a_all, w_all, sems = refs[-4:]
    half = w_all.shape[1]
    place, _, here = coordinates()
    columns = pl.ds(pl.multiple_of(here // 2 * half, half), half)
    gather_rows(place, refs[:-4], w_ref.at[:, columns], a_all, w_all, sems)
    out_ref[...] = jnp.dot(a_all[...], w_all[...], preferred_element_type=jnp.float32)


def far_kernel(w_ref, near_ref, *refs):
    place, _, here = coordinates()
    mine_ref, other_ref, a_all, w_all, total, sems = refs[-6:]
    gather_rows(place, refs[:-6], w_ref, a_all, w_all, sems)
    total[...] = near_ref[...] + jnp.dot(a_all[...], w_all[...], preferred_element_type=jnp.float32)
    width = mine_ref.shape[1]
    core = here % 2
    mine_ref[...] = total[:, pl.ds(pl.multiple_of(core * width, width), width)]
    other_ref[...] = total[:, pl.ds(pl.multiple_of((1 - core) * width, width), width)].astype(jnp.bfloat16)


def near_sums(out_weight, pieces):
    rows, width = pieces[0].shape
    depth, half = out_weight.shape[0], out_weight.shape[1] // 2
    anywhere = pl.BlockSpec(memory_space=pl.ANY)
    return pl.pallas_call(
        near_kernel,
        out_shape=jax.ShapeDtypeStruct((rows, half), jnp.float32),
        in_specs=[anywhere] * (1 + len(pieces)),
        out_specs=pl.BlockSpec(memory_space=pltpu.VMEM),
        scratch_shapes=[
            pltpu.VMEM((rows, depth), jnp.bfloat16),
            pltpu.VMEM((depth, half), jnp.bfloat16),
            pltpu.SemaphoreType.DMA((1 + len(pieces),)),
        ],
        compiler_params=pltpu.CompilerParams(vmem_limit_bytes=24 * 1024 * 1024),
        cost_estimate=pl.CostEstimate(flops=1500000000, bytes_accessed=4950000, transcendentals=0),
        name="near_sums",
    )(out_weight, *pieces)


def far_sums(weights, near, pieces):
    rows, width = pieces[0].shape
    depth, half = weights.shape
    anywhere = pl.BlockSpec(memory_space=pl.ANY)
    local_memory = pl.BlockSpec(memory_space=pltpu.VMEM)
    return pl.pallas_call(
        far_kernel,
        out_shape=(
            jax.ShapeDtypeStruct((rows, half // 2), jnp.float32),
            jax.ShapeDtypeStruct((rows, half // 2), jnp.bfloat16),
        ),
        in_specs=[anywhere, local_memory] + [anywhere] * len(pieces),
        out_specs=(local_memory, local_memory),
        scratch_shapes=[
            pltpu.VMEM((rows, depth), jnp.bfloat16),
            pltpu.VMEM((depth, half), jnp.bfloat16),
            pltpu.VMEM((rows, half), jnp.float32),
            pltpu.SemaphoreType.DMA((1 + len(pieces),)),
        ],
        compiler_params=pltpu.CompilerParams(vmem_limit_bytes=24 * 1024 * 1024),
        cost_estimate=pl.CostEstimate(flops=1800000000, bytes_accessed=5940000, transcendentals=0),
        name="far_sums",
    )(weights, near, *pieces)


def head_plan(queries, keys, values, cluster_ids, out_weight):
    heads = cluster_ids.shape[0]
    here = lax.axis_index("head").astype(jnp.int32)

    def swap(array, axis, bits):
        size = lax.axis_size(axis)
        return lax.ppermute(array, axis, [(place, place ^ bits) for place in range(size)])

    def after(array, *others):
        return lax.optimization_barrier((array,) + others)[0]

    q, kv = pack(queries, keys, values, cluster_ids)
    kv_own, kv_far, q_own = [kv[0]] + [None] * 3, [None] * 4, [q[0]] + [None] * 3
    kv_own[2] = swap(kv[2], "seq", 4)
    kv_own[1] = swap(kv[1], "seq", 2)
    kv_far[0] = swap(kv[0], "seq", 1)
    kv_own[3] = swap(after(kv[3], kv_own[1]), "seq", 6)
    half = out_weight.shape[1] // 2
    weights = lax.dynamic_slice_in_dim(after(out_weight, kv[1]), (1 - here // 2) * half, half, 1)
    weights = swap(weights, "head", 2)
    for offset in (1, 2, 3):
        kv_far[offset] = swap(kv_own[offset], "seq", 1)
    q_own[2] = swap(after(q[2], kv_own[2]), "seq", 4)
    for offset in (3, 1):
        q_own[offset] = swap(after(q[offset], kv_own[3]), "seq", 2 * offset)
    attended = list(attend(kv_own, kv_far, q_own))
    for offset in range(1, heads):
        attended[offset] = swap(attended[offset], "seq", 2 * offset)
    across = [swap(piece, "head", 2) for piece in attended]
    near = near_sums(out_weight, attended)
    mine, other = far_sums(weights, near, across)
    return (mine + swap(other, "head", 1).astype(jnp.float32)).astype(jnp.bfloat16)


def local(queries, keys, values, cluster_ids, out_weight):
    groups = cluster_ids.shape[0]
    if lax.axis_size("seq") == 2 * groups and lax.axis_size("head") == 4:
        return head_plan(queries, keys, values, cluster_ids, out_weight)
    return padded_plan(queries, keys, values, cluster_ids, out_weight)


def solution(mesh):
    placed = (
        P("seq", "head"),
        P("seq", "head"),
        P("seq", "head"),
        P("head", "seq"),
        P("head", None),
    )
    return jax.shard_map(
        local, mesh=mesh, in_specs=placed, out_specs=P("seq", "head"), check_vma=False
    )
```

```python
import math

import jax
import jax.numpy as jnp
from jax import lax
from jax.experimental import pallas as pl
from jax.experimental.pallas import tpu as pltpu
from jax.sharding import PartitionSpec as P

CLUSTERS = 256
MOST = 4


def attend_block(query_part, key_part, value_part, filled_part, score_scale):
    owners, local_slots, head_width = query_part.shape
    local_count = filled_part.shape[1]
    slot_count = local_slots // local_count
    query_rows = query_part.reshape(owners, local_count, slot_count, head_width)
    key_rows = key_part.reshape(owners, local_count, slot_count, head_width)
    value_rows = value_part.reshape(owners, local_count, slot_count, head_width)
    scores = (
        jnp.einsum("scmd,tcnd->csmtn", query_rows, key_rows, preferred_element_type=jnp.float32)
        * score_scale
    )
    order_index = jnp.arange(owners * slot_count, dtype=jnp.int32).reshape(owners, slot_count)
    before = order_index[None, None, :, :] <= order_index[:, :, None, None]
    itself = order_index[None, None, :, :] == order_index[:, :, None, None]
    slot_value = jnp.arange(slot_count, dtype=jnp.float32)[None, None, :]
    taken_slot = slot_value < jnp.transpose(filled_part).astype(jnp.float32)[:, :, None]
    allowed = before[None] & (taken_slot[:, None, None, :, :] | itself[None])
    scores = jnp.where(allowed, scores, -1e30)
    row_top = jnp.max(scores, axis=(3, 4), keepdims=True)
    spread = jnp.exp(scores - row_top)
    weights = (spread / jnp.sum(spread, axis=(3, 4), keepdims=True)).astype(jnp.bfloat16)
    combined = jnp.einsum(
        "csmtn,tcnd->scmd", weights, value_rows, preferred_element_type=jnp.float32
    )
    return combined.astype(jnp.bfloat16).reshape(owners, local_slots, head_width)


def padded_plan(queries, keys, values, cluster_ids, out_weight):
    token_count = queries.shape[0]
    groups = cluster_ids.shape[0]
    head_width = queries.shape[1] // groups
    owners = lax.axis_size("seq")
    local_count = CLUSTERS // owners
    position = jnp.arange(token_count, dtype=jnp.int32)
    earlier = position[None, :] < position[:, None]
    matching = cluster_ids[:, :, None] == cluster_ids[:, None, :]
    slot_rank = jnp.sum((matching & earlier[None]).astype(jnp.int32), axis=2)
    owner_index = jnp.transpose(cluster_ids // local_count)
    within_owner = jnp.transpose(cluster_ids % local_count * MOST + slot_rank)
    head_index = jnp.arange(groups, dtype=jnp.int32)[None, :]

    def place(source):
        shaped = source.reshape(token_count, groups, head_width)
        blank = jnp.zeros((owners, groups, local_count * MOST, head_width), jnp.bfloat16)
        return blank.at[owner_index, head_index, within_owner].set(shaped)

    cluster_axis = jnp.arange(CLUSTERS, dtype=jnp.int32)
    filled = jnp.sum(
        (cluster_ids[:, :, None] == cluster_axis[None, None, :]).astype(jnp.int32), axis=1
    )
    filled = jnp.transpose(filled.reshape(groups, owners, local_count), (1, 0, 2)).astype(
        jnp.bfloat16
    )
    score_scale = 1.0 / math.sqrt(head_width)
    query_in = lax.all_to_all(place(queries), "seq", split_axis=0, concat_axis=0, tiled=True)
    key_in = lax.all_to_all(place(keys), "seq", split_axis=0, concat_axis=0, tiled=True)
    value_in = lax.all_to_all(place(values), "seq", split_axis=0, concat_axis=0, tiled=True)
    count_in = lax.all_to_all(filled, "seq", split_axis=0, concat_axis=0, tiled=True)

    def one_head(position_head):
        return attend_block(
            lax.dynamic_index_in_dim(query_in, position_head, 1, False),
            lax.dynamic_index_in_dim(key_in, position_head, 1, False),
            lax.dynamic_index_in_dim(value_in, position_head, 1, False),
            lax.dynamic_index_in_dim(count_in, position_head, 1, False),
            score_scale,
        )

    results = lax.map(one_head, jnp.arange(query_in.shape[1], dtype=jnp.int32))
    returned = lax.all_to_all(results, "seq", split_axis=1, concat_axis=1, tiled=True)
    gathered = returned[head_index, owner_index, within_owner]
    attended = gathered.reshape(token_count, groups * head_width)
    partial_sums = jnp.dot(attended, out_weight, preferred_element_type=jnp.float32)
    summed = lax.psum_scatter(partial_sums, "head", scatter_dimension=1, tiled=True)
    return summed.astype(jnp.bfloat16)


ID_ROWS = 16
MISMATCH = 262144.0


def coordinates():
    seq = lax.axis_index("seq").astype(jnp.int32)
    return seq // 2, seq % 2, lax.axis_index("head").astype(jnp.int32)


def pack_kernel(q_ref, k_ref, v_ref, ids_ref, *outs):
    heads = ids_ref.shape[0]
    rows, width = outs[0].shape
    parts = rows // width
    place = coordinates()[0]
    queries_out = [outs[0], outs[1].at[pl.ds(2 * rows + ID_ROWS, rows)]] + list(outs[2:heads])
    keys_out = [outs[heads], outs[1]] + list(outs[heads + 1 :])
    for offset in range(heads):
        q_out, kv_out = queries_out[offset], keys_out[offset]
        head = lax.bitwise_xor(place, offset)
        columns = pl.ds(pl.multiple_of(head * width, width), width)
        kv_out[pl.ds(0, rows), :] = k_ref[:, columns]
        kv_out[pl.ds(rows, rows), :] = v_ref[:, columns]
        q_out[...] = q_ref[:, columns]
        ids = ids_ref[pl.ds(head, 1), :].astype(jnp.float32)
        lines = [ids[:, part * width : (part + 1) * width] for part in range(parts)]
        lines.append(jnp.zeros((ID_ROWS - parts, width), jnp.float32))
        kv_out[pl.ds(2 * rows, ID_ROWS), :] = jnp.concatenate(lines, axis=0).astype(jnp.bfloat16)


def pack(queries, keys, values, cluster_ids):
    heads = cluster_ids.shape[0]
    rows = queries.shape[0]
    width = queries.shape[1] // heads
    local_memory = pl.BlockSpec(memory_space=pltpu.VMEM)
    sizes = [rows, 3 * rows + ID_ROWS] + [rows] * (heads - 2) + [2 * rows + ID_ROWS] * (heads - 1)
    outs = pl.pallas_call(
        pack_kernel,
        out_shape=tuple(jax.ShapeDtypeStruct((size, width), jnp.bfloat16) for size in sizes),
        in_specs=[local_memory] * 4,
        out_specs=(local_memory,) * len(sizes),
        cost_estimate=pl.CostEstimate(flops=2700000000, bytes_accessed=8910000, transcendentals=0),
        name="pack",
    )(queries, keys, values, cluster_ids)
    return list(outs[:heads]), [outs[heads], outs[1]] + list(outs[heads + 1 :])


def attend_kernel(scale, *refs):
    place, later, _ = coordinates()
    pieces = (len(refs) - 6) // 4
    own_refs, far_refs, q_refs, out_refs = (refs[pieces * kind : pieces * (kind + 1)] for kind in range(4))
    k_all, v_all, q_all, ids_all, out_all, sems = refs[4 * pieces :]
    rows, width = q_refs[0].shape
    parts = rows // width
    tile = 256
    slots = [lax.bitwise_xor(place, offset) for offset in range(pieces)]
    sides = (own_refs, far_refs)

    def copies_of(offset, slot):
        span = pl.ds(slot * rows if isinstance(slot, int) else pl.multiple_of(slot * rows, rows), rows)
        pairs = []
        for side, side_refs in enumerate(sides):
            ref = side_refs[offset]
            pairs.append((ref.at[pl.ds(2 * rows, ID_ROWS)], ids_all.at[side, slot]))
        source = q_refs[offset]
        if source.shape[0] > rows:
            source = source.at[pl.ds(2 * rows + ID_ROWS, rows)]
        pairs.append((source, q_all.at[span, pl.ds(0, width)]))
        for side, side_refs in enumerate(sides):
            ref = side_refs[offset]
            pairs.append((ref.at[pl.ds(0, rows)], k_all.at[side, span, pl.ds(0, width)]))
            pairs.append((ref.at[pl.ds(rows, rows)], v_all.at[side, span, pl.ds(0, width)]))
        return [
            pltpu.make_async_copy(source, target, sems.at[kind, slot]) for kind, (source, target) in enumerate(pairs)
        ]

    for offset, slot in enumerate(slots):
        for copy in copies_of(offset, slot):
            copy.start()
    v_all[:, :, width:] = jnp.ones((2, pieces * rows, width), jnp.bfloat16)
    lane = lax.broadcasted_iota(jnp.int32, (width, width), 1)
    shift = jnp.minimum(lane // 2, 8)
    odd = lane % 2
    live = lane < 16
    far_bias = jnp.where(later > 0, 0.0, -MISMATCH * 4.0).astype(jnp.float32)
    factor = scale * math.log2(math.e)
    contract = (((1,), (1,)), ((), ()))
    row = lax.broadcasted_iota(jnp.int32, (tile, tile), 0)
    column = lax.broadcasted_iota(jnp.int32, (tile, tile), 1)

    def ready(piece):
        waits = copies_of(0, piece)
        for copy in waits[:2]:
            copy.wait()
        for side in range(2):
            ids = ids_all[side, piece].astype(jnp.float32)
            for part in range(parts):
                line = jnp.broadcast_to(ids[part : part + 1], (width, width)).T.astype(jnp.int32)
                flag = lax.bitwise_xor(lax.bitwise_and(lax.shift_right_logical(line, shift), 1), odd)
                here = pl.ds(piece * rows + part * width, width)
                mark = jnp.where(live, flag.astype(jnp.float32), 0.0)
                k_all[side, here, width:] = mark.astype(jnp.bfloat16)
                if side == 0:
                    other = jnp.where(live, (flag.astype(jnp.float32) - 1.0) * MISMATCH, 0.0)
                    q_all[here, width:] = other.astype(jnp.bfloat16)
        for copy in waits[2:]:
            copy.wait()

    def scores_of(piece, step):
        edge = piece * rows + step * tile
        q = q_all[pl.ds(edge, tile), :]
        own = lax.dot_general(q, k_all[0, pl.ds(0, edge + tile), :], contract, preferred_element_type=jnp.float32)
        far = lax.dot_general(
            q, k_all[1, pl.ds(0, (piece + 1) * rows), :], contract, preferred_element_type=jnp.float32
        )
        return own, far

    def finish(piece, step, own, far):
        before = piece * rows
        edge = before + step * tile
        diagonal = jnp.where(column <= row, own[:, edge:], -MISMATCH * 4.0)
        last = far[:, before:] + far_bias
        own = jnp.concatenate([own[:, :edge], diagonal], axis=1) if edge else diagonal
        far = jnp.concatenate([far[:, :before], last], axis=1) if before else last
        top = own[:, :width]
        for start in range(width, own.shape[1], width):
            top = jnp.maximum(top, own[:, start : start + width])
        for start in range(0, far.shape[1], width):
            top = jnp.maximum(top, far[:, start : start + width])
        top = jnp.max(top, axis=1, keepdims=True) * factor
        own = jnp.exp2(own * factor - top).astype(jnp.bfloat16)
        far = jnp.exp2(far * factor - top).astype(jnp.bfloat16)
        total = jnp.dot(own, v_all[0, pl.ds(0, own.shape[1]), :], preferred_element_type=jnp.float32)
        total = total + jnp.dot(far, v_all[1, pl.ds(0, far.shape[1]), :], preferred_element_type=jnp.float32)
        result = total[:, :width] / total[:, width:]
        out_all[piece, pl.ds(step * tile, tile), :] = result.astype(jnp.bfloat16)

    pending = None
    for piece in range(pieces):
        ready(piece)
    for piece in range(pieces):
        for step in range(rows // tile):
            scores = scores_of(piece, step)
            if pending is not None:
                finish(*pending)
            pending = (piece, step) + scores
    finish(*pending)
    copies = [
        pltpu.make_async_copy(out_all.at[slot], ref, sems.at[0, offset])
        for offset, (slot, ref) in enumerate(zip(slots, out_refs))
    ]
    for copy in copies:
        copy.start()
    for copy in copies:
        copy.wait()


def attend(kv_own, kv_far, q):
    pieces = len(q)
    rows, width = q[0].shape
    anywhere = pl.BlockSpec(memory_space=pl.ANY)
    return pl.pallas_call(
        lambda *refs: attend_kernel(1.0 / math.sqrt(width), *refs),
        out_shape=(jax.ShapeDtypeStruct((rows, width), jnp.bfloat16),) * pieces,
        in_specs=[anywhere] * (3 * pieces),
        out_specs=(anywhere,) * pieces,
        scratch_shapes=[
            pltpu.VMEM((2, pieces * rows, 2 * width), jnp.bfloat16),
            pltpu.VMEM((2, pieces * rows, 2 * width), jnp.bfloat16),
            pltpu.VMEM((pieces * rows, 2 * width), jnp.bfloat16),
            pltpu.VMEM((2, pieces, ID_ROWS, width), jnp.bfloat16),
            pltpu.VMEM((pieces, rows, width), jnp.bfloat16),
            pltpu.SemaphoreType.DMA((7, pieces)),
        ],
        compiler_params=pltpu.CompilerParams(vmem_limit_bytes=48 * 1024 * 1024),
        cost_estimate=pl.CostEstimate(flops=4000000000, bytes_accessed=13200000, transcendentals=0),
        name="attend",
    )(*kv_own, *kv_far, *q)


def gather_rows(place, pieces, w_source, a_all, w_all, sems):
    rows, width = pieces[0].shape
    copies = [pltpu.make_async_copy(w_source, w_all, sems.at[len(pieces)])]
    for offset, ref in enumerate(pieces):
        head = lax.bitwise_xor(place, offset)
        columns = pl.ds(pl.multiple_of(head * width, width), width)
        copies.append(pltpu.make_async_copy(ref, a_all.at[:, columns], sems.at[offset]))
    for copy in copies:
        copy.start()
    for copy in copies:
        copy.wait()


def near_kernel(w_ref, *refs):
    out_ref, a_all, w_all, sems = refs[-4:]
    half = w_all.shape[1]
    place, _, here = coordinates()
    columns = pl.ds(pl.multiple_of(here // 2 * half, half), half)
    gather_rows(place, refs[:-4], w_ref.at[:, columns], a_all, w_all, sems)
    out_ref[...] = jnp.dot(a_all[...], w_all[...], preferred_element_type=jnp.float32)


def far_kernel(w_ref, near_ref, *refs):
    place, _, here = coordinates()
    mine_ref, other_ref, a_all, w_all, total, sems = refs[-6:]
    gather_rows(place, refs[:-6], w_ref, a_all, w_all, sems)
    total[...] = near_ref[...] + jnp.dot(a_all[...], w_all[...], preferred_element_type=jnp.float32)
    width = mine_ref.shape[1]
    core = here % 2
    mine_ref[...] = total[:, pl.ds(pl.multiple_of(core * width, width), width)]
    other_ref[...] = total[:, pl.ds(pl.multiple_of((1 - core) * width, width), width)].astype(jnp.bfloat16)


def near_sums(out_weight, pieces):
    rows, width = pieces[0].shape
    depth, half = out_weight.shape[0], out_weight.shape[1] // 2
    anywhere = pl.BlockSpec(memory_space=pl.ANY)
    return pl.pallas_call(
        near_kernel,
        out_shape=jax.ShapeDtypeStruct((rows, half), jnp.float32),
        in_specs=[anywhere] * (1 + len(pieces)),
        out_specs=pl.BlockSpec(memory_space=pltpu.VMEM),
        scratch_shapes=[
            pltpu.VMEM((rows, depth), jnp.bfloat16),
            pltpu.VMEM((depth, half), jnp.bfloat16),
            pltpu.SemaphoreType.DMA((1 + len(pieces),)),
        ],
        compiler_params=pltpu.CompilerParams(vmem_limit_bytes=24 * 1024 * 1024),
        cost_estimate=pl.CostEstimate(flops=1500000000, bytes_accessed=4950000, transcendentals=0),
        name="near_sums",
    )(out_weight, *pieces)


def far_sums(weights, near, pieces):
    rows, width = pieces[0].shape
    depth, half = weights.shape
    anywhere = pl.BlockSpec(memory_space=pl.ANY)
    local_memory = pl.BlockSpec(memory_space=pltpu.VMEM)
    return pl.pallas_call(
        far_kernel,
        out_shape=(
            jax.ShapeDtypeStruct((rows, half // 2), jnp.float32),
            jax.ShapeDtypeStruct((rows, half // 2), jnp.bfloat16),
        ),
        in_specs=[anywhere, local_memory] + [anywhere] * len(pieces),
        out_specs=(local_memory, local_memory),
        scratch_shapes=[
            pltpu.VMEM((rows, depth), jnp.bfloat16),
            pltpu.VMEM((depth, half), jnp.bfloat16),
            pltpu.VMEM((rows, half), jnp.float32),
            pltpu.SemaphoreType.DMA((1 + len(pieces),)),
        ],
        compiler_params=pltpu.CompilerParams(vmem_limit_bytes=24 * 1024 * 1024),
        cost_estimate=pl.CostEstimate(flops=1800000000, bytes_accessed=5940000, transcendentals=0),
        name="far_sums",
    )(weights, near, *pieces)


def head_plan(queries, keys, values, cluster_ids, out_weight):
    heads = cluster_ids.shape[0]
    here = lax.axis_index("head").astype(jnp.int32)

    def swap(array, axis, bits):
        size = lax.axis_size(axis)
        return lax.ppermute(array, axis, [(place, place ^ bits) for place in range(size)])

    def after(array, *others):
        return lax.optimization_barrier((array,) + others)[0]

    q, kv = pack(queries, keys, values, cluster_ids)
    kv_own, kv_far, q_own = [kv[0]] + [None] * 3, [None] * 4, [q[0]] + [None] * 3
    kv_own[2] = swap(kv[2], "seq", 4)
    kv_own[1] = swap(kv[1], "seq", 2)
    kv_far[0] = swap(kv[0], "seq", 1)
    kv_own[3] = swap(after(kv[3], kv_own[2]), "seq", 6)
    half = out_weight.shape[1] // 2
    weights = lax.dynamic_slice_in_dim(after(out_weight, kv[1]), (1 - here // 2) * half, half, 1)
    weights = swap(weights, "head", 2)
    q_own[1] = kv_own[1]
    kv_far[1] = swap(kv_own[1][: kv[0].shape[0]], "seq", 1)
    for offset in (2, 3):
        kv_far[offset] = swap(kv_own[offset], "seq", 1)
    q_own[2] = swap(after(q[2], kv_own[2]), "seq", 4)
    q_own[3] = swap(after(q[3], kv_own[2]), "seq", 6)
    attended = list(attend(kv_own, kv_far, q_own))
    for offset in range(1, heads):
        attended[offset] = swap(attended[offset], "seq", 2 * offset)
    across = [swap(piece, "head", 2) for piece in attended]
    near = near_sums(out_weight, attended)
    mine, other = far_sums(weights, near, across)
    return (mine + swap(other, "head", 1).astype(jnp.float32)).astype(jnp.bfloat16)


def local(queries, keys, values, cluster_ids, out_weight):
    groups = cluster_ids.shape[0]
    if lax.axis_size("seq") == 2 * groups and lax.axis_size("head") == 4:
        return head_plan(queries, keys, values, cluster_ids, out_weight)
    return padded_plan(queries, keys, values, cluster_ids, out_weight)


def solution(mesh):
    placed = (
        P("seq", "head"),
        P("seq", "head"),
        P("seq", "head"),
        P("head", "seq"),
        P("head", None),
    )
    return jax.shard_map(
        local, mesh=mesh, in_specs=placed, out_specs=P("seq", "head"), check_vma=False
    )
```

```python
import math

import jax
import jax.numpy as jnp
from jax import lax
from jax.experimental import pallas as pl
from jax.experimental.pallas import tpu as pltpu
from jax.sharding import PartitionSpec as P

CLUSTERS = 256
MOST = 4


def attend_block(query_part, key_part, value_part, filled_part, score_scale):
    owners, local_slots, head_width = query_part.shape
    local_count = filled_part.shape[1]
    slot_count = local_slots // local_count
    query_rows = query_part.reshape(owners, local_count, slot_count, head_width)
    key_rows = key_part.reshape(owners, local_count, slot_count, head_width)
    value_rows = value_part.reshape(owners, local_count, slot_count, head_width)
    scores = (
        jnp.einsum("scmd,tcnd->csmtn", query_rows, key_rows, preferred_element_type=jnp.float32)
        * score_scale
    )
    order_index = jnp.arange(owners * slot_count, dtype=jnp.int32).reshape(owners, slot_count)
    before = order_index[None, None, :, :] <= order_index[:, :, None, None]
    itself = order_index[None, None, :, :] == order_index[:, :, None, None]
    slot_value = jnp.arange(slot_count, dtype=jnp.float32)[None, None, :]
    taken_slot = slot_value < jnp.transpose(filled_part).astype(jnp.float32)[:, :, None]
    allowed = before[None] & (taken_slot[:, None, None, :, :] | itself[None])
    scores = jnp.where(allowed, scores, -1e30)
    row_top = jnp.max(scores, axis=(3, 4), keepdims=True)
    spread = jnp.exp(scores - row_top)
    weights = (spread / jnp.sum(spread, axis=(3, 4), keepdims=True)).astype(jnp.bfloat16)
    combined = jnp.einsum(
        "csmtn,tcnd->scmd", weights, value_rows, preferred_element_type=jnp.float32
    )
    return combined.astype(jnp.bfloat16).reshape(owners, local_slots, head_width)


def padded_plan(queries, keys, values, cluster_ids, out_weight):
    token_count = queries.shape[0]
    groups = cluster_ids.shape[0]
    head_width = queries.shape[1] // groups
    owners = lax.axis_size("seq")
    local_count = CLUSTERS // owners
    position = jnp.arange(token_count, dtype=jnp.int32)
    earlier = position[None, :] < position[:, None]
    matching = cluster_ids[:, :, None] == cluster_ids[:, None, :]
    slot_rank = jnp.sum((matching & earlier[None]).astype(jnp.int32), axis=2)
    owner_index = jnp.transpose(cluster_ids // local_count)
    within_owner = jnp.transpose(cluster_ids % local_count * MOST + slot_rank)
    head_index = jnp.arange(groups, dtype=jnp.int32)[None, :]

    def place(source):
        shaped = source.reshape(token_count, groups, head_width)
        blank = jnp.zeros((owners, groups, local_count * MOST, head_width), jnp.bfloat16)
        return blank.at[owner_index, head_index, within_owner].set(shaped)

    cluster_axis = jnp.arange(CLUSTERS, dtype=jnp.int32)
    filled = jnp.sum(
        (cluster_ids[:, :, None] == cluster_axis[None, None, :]).astype(jnp.int32), axis=1
    )
    filled = jnp.transpose(filled.reshape(groups, owners, local_count), (1, 0, 2)).astype(
        jnp.bfloat16
    )
    score_scale = 1.0 / math.sqrt(head_width)
    query_in = lax.all_to_all(place(queries), "seq", split_axis=0, concat_axis=0, tiled=True)
    key_in = lax.all_to_all(place(keys), "seq", split_axis=0, concat_axis=0, tiled=True)
    value_in = lax.all_to_all(place(values), "seq", split_axis=0, concat_axis=0, tiled=True)
    count_in = lax.all_to_all(filled, "seq", split_axis=0, concat_axis=0, tiled=True)

    def one_head(position_head):
        return attend_block(
            lax.dynamic_index_in_dim(query_in, position_head, 1, False),
            lax.dynamic_index_in_dim(key_in, position_head, 1, False),
            lax.dynamic_index_in_dim(value_in, position_head, 1, False),
            lax.dynamic_index_in_dim(count_in, position_head, 1, False),
            score_scale,
        )

    results = lax.map(one_head, jnp.arange(query_in.shape[1], dtype=jnp.int32))
    returned = lax.all_to_all(results, "seq", split_axis=1, concat_axis=1, tiled=True)
    gathered = returned[head_index, owner_index, within_owner]
    attended = gathered.reshape(token_count, groups * head_width)
    partial_sums = jnp.dot(attended, out_weight, preferred_element_type=jnp.float32)
    summed = lax.psum_scatter(partial_sums, "head", scatter_dimension=1, tiled=True)
    return summed.astype(jnp.bfloat16)


ID_ROWS = 16
MISMATCH = 262144.0


def coordinates():
    seq = lax.axis_index("seq").astype(jnp.int32)
    return seq // 2, seq % 2, lax.axis_index("head").astype(jnp.int32)


def pack_kernel(q_ref, k_ref, v_ref, ids_ref, *outs):
    heads = ids_ref.shape[0]
    rows, width = outs[0].shape
    parts = rows // width
    place = coordinates()[0]
    queries_out = [outs[0], outs[1].at[pl.ds(2 * rows + ID_ROWS, rows)]] + list(outs[2:heads])
    keys_out = [outs[heads], outs[1]] + list(outs[heads + 1 :])
    for offset in range(heads):
        q_out, kv_out = queries_out[offset], keys_out[offset]
        head = lax.bitwise_xor(place, offset)
        columns = pl.ds(pl.multiple_of(head * width, width), width)
        kv_out[pl.ds(0, rows), :] = k_ref[:, columns]
        kv_out[pl.ds(rows, rows), :] = v_ref[:, columns]
        q_out[...] = q_ref[:, columns]
        ids = ids_ref[pl.ds(head, 1), :].astype(jnp.float32)
        lines = [ids[:, part * width : (part + 1) * width] for part in range(parts)]
        lines.append(jnp.zeros((ID_ROWS - parts, width), jnp.float32))
        kv_out[pl.ds(2 * rows, ID_ROWS), :] = jnp.concatenate(lines, axis=0).astype(jnp.bfloat16)


def pack(queries, keys, values, cluster_ids):
    heads = cluster_ids.shape[0]
    rows = queries.shape[0]
    width = queries.shape[1] // heads
    local_memory = pl.BlockSpec(memory_space=pltpu.VMEM)
    sizes = [rows, 3 * rows + ID_ROWS] + [rows] * (heads - 2) + [2 * rows + ID_ROWS] * (heads - 1)
    outs = pl.pallas_call(
        pack_kernel,
        out_shape=tuple(jax.ShapeDtypeStruct((size, width), jnp.bfloat16) for size in sizes),
        in_specs=[local_memory] * 4,
        out_specs=(local_memory,) * len(sizes),
        cost_estimate=pl.CostEstimate(flops=2700000000, bytes_accessed=8910000, transcendentals=0),
        name="pack",
    )(queries, keys, values, cluster_ids)
    return list(outs[:heads]), [outs[heads], outs[1]] + list(outs[heads + 1 :])


def attend_kernel(scale, *refs):
    place, later, _ = coordinates()
    pieces = (len(refs) - 6) // 4
    own_refs, far_refs, q_refs, out_refs = (refs[pieces * kind : pieces * (kind + 1)] for kind in range(4))
    k_all, v_all, q_all, ids_all, out_all, sems = refs[4 * pieces :]
    rows, width = q_refs[0].shape
    parts = rows // width
    tile = 256
    slots = [lax.bitwise_xor(place, offset) for offset in range(pieces)]
    sides = (own_refs, far_refs)

    def copies_of(offset, slot):
        span = pl.ds(slot * rows if isinstance(slot, int) else pl.multiple_of(slot * rows, rows), rows)
        pairs = []
        for side, side_refs in enumerate(sides):
            ref = side_refs[offset]
            pairs.append((ref.at[pl.ds(2 * rows, ID_ROWS)], ids_all.at[side, slot]))
        source = q_refs[offset]
        if source.shape[0] > rows:
            source = source.at[pl.ds(2 * rows + ID_ROWS, rows)]
        pairs.append((source, q_all.at[span, pl.ds(0, width)]))
        for side, side_refs in enumerate(sides):
            ref = side_refs[offset]
            pairs.append((ref.at[pl.ds(0, rows)], k_all.at[side, span, pl.ds(0, width)]))
            pairs.append((ref.at[pl.ds(rows, rows)], v_all.at[side, span, pl.ds(0, width)]))
        return [
            pltpu.make_async_copy(source, target, sems.at[kind, slot]) for kind, (source, target) in enumerate(pairs)
        ]

    for offset, slot in enumerate(slots):
        for copy in copies_of(offset, slot):
            copy.start()
    v_all[:, :, width:] = jnp.ones((2, pieces * rows, width), jnp.bfloat16)
    lane = lax.broadcasted_iota(jnp.int32, (width, width), 1)
    shift = jnp.minimum(lane // 2, 8)
    odd = lane % 2
    live = lane < 16
    far_bias = jnp.where(later > 0, 0.0, -MISMATCH * 4.0).astype(jnp.float32)
    factor = scale * math.log2(math.e)
    contract = (((1,), (1,)), ((), ()))
    row = lax.broadcasted_iota(jnp.int32, (tile, tile), 0)
    column = lax.broadcasted_iota(jnp.int32, (tile, tile), 1)

    def ready(piece):
        waits = copies_of(0, piece)
        for copy in waits[:2]:
            copy.wait()
        for side in range(2):
            ids = ids_all[side, piece].astype(jnp.float32)
            for part in range(parts):
                line = jnp.broadcast_to(ids[part : part + 1], (width, width)).T.astype(jnp.int32)
                flag = lax.bitwise_xor(lax.bitwise_and(lax.shift_right_logical(line, shift), 1), odd)
                here = pl.ds(piece * rows + part * width, width)
                mark = jnp.where(live, flag.astype(jnp.float32), 0.0)
                k_all[side, here, width:] = mark.astype(jnp.bfloat16)
                if side == 0:
                    other = jnp.where(live, (flag.astype(jnp.float32) - 1.0) * MISMATCH, 0.0)
                    q_all[here, width:] = other.astype(jnp.bfloat16)
        for copy in waits[2:]:
            copy.wait()

    def scores_of(piece, step):
        edge = piece * rows + step * tile
        q = q_all[pl.ds(edge, tile), :]
        own = lax.dot_general(q, k_all[0, pl.ds(0, edge + tile), :], contract, preferred_element_type=jnp.float32)
        far = lax.dot_general(
            q, k_all[1, pl.ds(0, (piece + 1) * rows), :], contract, preferred_element_type=jnp.float32
        )
        return own, far

    def finish(piece, step, own, far):
        before = piece * rows
        edge = before + step * tile
        diagonal = jnp.where(column <= row, own[:, edge:], -MISMATCH * 4.0)
        last = far[:, before:] + far_bias
        own = jnp.concatenate([own[:, :edge], diagonal], axis=1) if edge else diagonal
        far = jnp.concatenate([far[:, :before], last], axis=1) if before else last
        top = own[:, :width]
        for start in range(width, own.shape[1], width):
            top = jnp.maximum(top, own[:, start : start + width])
        for start in range(0, far.shape[1], width):
            top = jnp.maximum(top, far[:, start : start + width])
        top = jnp.max(top, axis=1, keepdims=True) * factor
        own = jnp.exp2(own * factor - top).astype(jnp.bfloat16)
        far = jnp.exp2(far * factor - top).astype(jnp.bfloat16)
        total = jnp.dot(own, v_all[0, pl.ds(0, own.shape[1]), :], preferred_element_type=jnp.float32)
        total = total + jnp.dot(far, v_all[1, pl.ds(0, far.shape[1]), :], preferred_element_type=jnp.float32)
        result = total[:, :width] / total[:, width:]
        out_all[piece, pl.ds(step * tile, tile), :] = result.astype(jnp.bfloat16)

    pending = None
    for piece in range(pieces):
        ready(piece)
    for piece in range(pieces):
        for step in range(rows // tile):
            scores = scores_of(piece, step)
            if pending is not None:
                finish(*pending)
            pending = (piece, step) + scores
    finish(*pending)
    copies = [
        pltpu.make_async_copy(out_all.at[slot], ref, sems.at[0, offset])
        for offset, (slot, ref) in enumerate(zip(slots, out_refs))
    ]
    for copy in copies:
        copy.start()
    for copy in copies:
        copy.wait()


def attend(kv_own, kv_far, q):
    pieces = len(q)
    rows, width = q[0].shape
    anywhere = pl.BlockSpec(memory_space=pl.ANY)
    return pl.pallas_call(
        lambda *refs: attend_kernel(1.0 / math.sqrt(width), *refs),
        out_shape=(jax.ShapeDtypeStruct((rows, width), jnp.bfloat16),) * pieces,
        in_specs=[anywhere] * (3 * pieces),
        out_specs=(anywhere,) * pieces,
        scratch_shapes=[
            pltpu.VMEM((2, pieces * rows, 2 * width), jnp.bfloat16),
            pltpu.VMEM((2, pieces * rows, 2 * width), jnp.bfloat16),
            pltpu.VMEM((pieces * rows, 2 * width), jnp.bfloat16),
            pltpu.VMEM((2, pieces, ID_ROWS, width), jnp.bfloat16),
            pltpu.VMEM((pieces, rows, width), jnp.bfloat16),
            pltpu.SemaphoreType.DMA((7, pieces)),
        ],
        compiler_params=pltpu.CompilerParams(vmem_limit_bytes=48 * 1024 * 1024),
        cost_estimate=pl.CostEstimate(flops=4000000000, bytes_accessed=13200000, transcendentals=0),
        name="attend",
    )(*kv_own, *kv_far, *q)


def gather_rows(place, pieces, w_source, a_all, w_all, sems):
    rows, width = pieces[0].shape
    copies = [pltpu.make_async_copy(w_source, w_all, sems.at[len(pieces)])]
    for offset, ref in enumerate(pieces):
        head = lax.bitwise_xor(place, offset)
        columns = pl.ds(pl.multiple_of(head * width, width), width)
        copies.append(pltpu.make_async_copy(ref, a_all.at[:, columns], sems.at[offset]))
    for copy in copies:
        copy.start()
    for copy in copies:
        copy.wait()


def near_kernel(w_ref, *refs):
    out_ref, a_all, w_all, sems = refs[-4:]
    half = w_all.shape[1]
    place, _, here = coordinates()
    columns = pl.ds(pl.multiple_of(here // 2 * half, half), half)
    gather_rows(place, refs[:-4], w_ref.at[:, columns], a_all, w_all, sems)
    out_ref[...] = jnp.dot(a_all[...], w_all[...], preferred_element_type=jnp.float32)


def far_kernel(w_ref, near_ref, *refs):
    place, _, here = coordinates()
    mine_ref, other_ref, a_all, w_all, total, sems = refs[-6:]
    gather_rows(place, refs[:-6], w_ref, a_all, w_all, sems)
    total[...] = near_ref[...] + jnp.dot(a_all[...], w_all[...], preferred_element_type=jnp.float32)
    width = mine_ref.shape[1]
    core = here % 2
    mine_ref[...] = total[:, pl.ds(pl.multiple_of(core * width, width), width)]
    other_ref[...] = total[:, pl.ds(pl.multiple_of((1 - core) * width, width), width)].astype(jnp.bfloat16)


def near_sums(out_weight, pieces):
    rows, width = pieces[0].shape
    depth, half = out_weight.shape[0], out_weight.shape[1] // 2
    anywhere = pl.BlockSpec(memory_space=pl.ANY)
    return pl.pallas_call(
        near_kernel,
        out_shape=jax.ShapeDtypeStruct((rows, half), jnp.float32),
        in_specs=[anywhere] * (1 + len(pieces)),
        out_specs=pl.BlockSpec(memory_space=pltpu.VMEM),
        scratch_shapes=[
            pltpu.VMEM((rows, depth), jnp.bfloat16),
            pltpu.VMEM((depth, half), jnp.bfloat16),
            pltpu.SemaphoreType.DMA((1 + len(pieces),)),
        ],
        compiler_params=pltpu.CompilerParams(vmem_limit_bytes=24 * 1024 * 1024),
        cost_estimate=pl.CostEstimate(flops=1500000000, bytes_accessed=4950000, transcendentals=0),
        name="near_sums",
    )(out_weight, *pieces)


def far_sums(weights, near, pieces):
    rows, width = pieces[0].shape
    depth, half = weights.shape
    anywhere = pl.BlockSpec(memory_space=pl.ANY)
    local_memory = pl.BlockSpec(memory_space=pltpu.VMEM)
    return pl.pallas_call(
        far_kernel,
        out_shape=(
            jax.ShapeDtypeStruct((rows, half // 2), jnp.float32),
            jax.ShapeDtypeStruct((rows, half // 2), jnp.bfloat16),
        ),
        in_specs=[anywhere, local_memory] + [anywhere] * len(pieces),
        out_specs=(local_memory, local_memory),
        scratch_shapes=[
            pltpu.VMEM((rows, depth), jnp.bfloat16),
            pltpu.VMEM((depth, half), jnp.bfloat16),
            pltpu.VMEM((rows, half), jnp.float32),
            pltpu.SemaphoreType.DMA((1 + len(pieces),)),
        ],
        compiler_params=pltpu.CompilerParams(vmem_limit_bytes=24 * 1024 * 1024),
        cost_estimate=pl.CostEstimate(flops=1800000000, bytes_accessed=5940000, transcendentals=0),
        name="far_sums",
    )(weights, near, *pieces)


def head_plan(queries, keys, values, cluster_ids, out_weight):
    heads = cluster_ids.shape[0]
    here = lax.axis_index("head").astype(jnp.int32)

    def swap(array, axis, bits):
        size = lax.axis_size(axis)
        return lax.ppermute(array, axis, [(place, place ^ bits) for place in range(size)])

    def after(array, *others):
        return lax.optimization_barrier((array,) + others)[0]

    q, kv = pack(queries, keys, values, cluster_ids)
    kv_own, kv_far, q_own = [kv[0]] + [None] * 3, [None] * 4, [q[0]] + [None] * 3
    kv_own[2] = swap(kv[2], "seq", 4)
    kv_own[1] = swap(kv[1], "seq", 2)
    kv_far[0] = swap(kv[0], "seq", 1)
    kv_own[3] = swap(after(kv[3], kv_own[2], kv_far[0]), "seq", 6)
    half = out_weight.shape[1] // 2
    weights = lax.dynamic_slice_in_dim(after(out_weight, kv[1]), (1 - here // 2) * half, half, 1)
    weights = swap(weights, "head", 2)
    q_own[1] = kv_own[1]
    kv_far[1] = swap(kv_own[1][: kv[0].shape[0]], "seq", 1)
    for offset in (2, 3):
        kv_far[offset] = swap(kv_own[offset], "seq", 1)
    q_own[2] = swap(after(q[2], kv_own[2]), "seq", 4)
    q_own[3] = swap(after(q[3], kv_own[2]), "seq", 6)
    attended = list(attend(kv_own, kv_far, q_own))
    for offset in range(1, heads):
        attended[offset] = swap(attended[offset], "seq", 2 * offset)
    across = [swap(piece, "head", 2) for piece in attended]
    near = near_sums(out_weight, attended)
    mine, other = far_sums(weights, near, across)
    return (mine + swap(other, "head", 1).astype(jnp.float32)).astype(jnp.bfloat16)


def local(queries, keys, values, cluster_ids, out_weight):
    groups = cluster_ids.shape[0]
    if lax.axis_size("seq") == 2 * groups and lax.axis_size("head") == 4:
        return head_plan(queries, keys, values, cluster_ids, out_weight)
    return padded_plan(queries, keys, values, cluster_ids, out_weight)


def solution(mesh):
    placed = (
        P("seq", "head"),
        P("seq", "head"),
        P("seq", "head"),
        P("head", "seq"),
        P("head", None),
    )
    return jax.shard_map(
        local, mesh=mesh, in_specs=placed, out_specs=P("seq", "head"), check_vma=False
    )
```
